128 devices in a mesh: group: 8 (over x, core), local: 16 (over z, y).
Axes of the slice: x: 4, y: 4, z: 4, core: 2. Of those that a mesh axis runs over, the one named last changes fastest.
Arguments:
- tokens: bfloat16 [1024, 7168], P(('group', 'local')), may hold values from -6 to 6
- picked_group_index: int32 [1024, 4], P(('group', 'local')), may hold values from 0 to 7, as said below
- picked_expert_index: int32 [1024, 8], P(('group', 'local')), may hold values from 0 to 23, as said below
- routing_pick_weight: bfloat16 [1024, 8], P(('group', 'local')), may hold values from 0.099609375 to 0.59765625
- common_gate_weight: bfloat16 [7168, 2048], P(None, 'local'), may hold values from -0.0625 to 0.0625
- common_up_weight: bfloat16 [7168, 2048], P(None, 'local'), may hold values from -0.0625 to 0.0625
- common_down_weight: bfloat16 [2048, 7168], P('local'), may hold values from -0.125 to 0.125
- routed_gate_weight: bfloat16 [24, 7168, 2048], P('group', None, 'local'), may hold values from -0.0625 to 0.0625
- routed_up_weight: bfloat16 [24, 7168, 2048], P('group', None, 'local'), may hold values from -0.0625 to 0.0625
- routed_down_weight: bfloat16 [24, 2048, 7168], P('group', 'local'), may hold values from -0.125 to 0.125
- gate_block_scales: float32 [24, 56, 16], P('group', None, 'local'), may hold values from 0.5 to 2
- up_block_scales: float32 [24, 56, 16], P('group', None, 'local'), may hold values from 0.5 to 2
- down_block_scales: float32 [24, 16, 56], P('group', 'local'), may hold values from 0.5 to 2
- adapter_input_maps: bfloat16 [24, 7168, 32], P('group'), may hold values from -0.0625 to 0.0625
- adapter_output_maps: bfloat16 [24, 2, 16, 2048], P('group', None, None, 'local'), may hold values from -1.5 to 1.5
- adapter_down_input: bfloat16 [24, 2048, 16], P('group', 'local'), may hold values from -0.125 to 0.125
- adapter_down_output: bfloat16 [24, 16, 7168], P('group'), may hold values from -1.5 to 1.5
Outputs:
- mixed: bfloat16 [1024, 7168], P(('group', 'local'))
The draws below stay inside these ranges and needn't reach their ends.
Inputs may be any that keep to these rules, and one draw needn't show every extreme that they name: `picked_group_index`: each row names 4 different groups. Among the rows of one device every group is named by exactly 4 rows. `picked_expert_index`: each row names 8 different experts, each in a group that the same row of picked_group_index names.
All inputs are finite; a program needn't handle non-finite values.
Results may differ from the reference program's by a relative error of at most 0.02.
Values may be sent and summed in bfloat16 or wider, within the bound.
A program may use at most 128 MiB of HBM per device.

```python
import math
import jax
import jax.numpy as jnp
from jax import lax

MODEL_WIDTH = 7168
EXPERT_HIDDEN = 2048
SH_FF = 2048
TOPK = 8
TOPK_GROUP = 4
ADAPTER_RANK = 16
QB = 128
EPG = 3
TOK_DEV = 8
GCAP = 4
TOKENS = 1024
ROUTED_EXPERTS = 24
N_GROUP = 8
N_LOCAL = 16


def routing_draws(key):
    device_total = TOKENS // TOK_DEV
    key_list = jax.random.split(key, 5)
    hot_column = jax.random.randint(key_list[0], (N_LOCAL,), 0, N_GROUP).astype(jnp.int32)
    hot_group = jnp.tile(hot_column, device_total // N_LOCAL)
    token_rank = jax.vmap(lambda sub_key: jax.random.permutation(sub_key, TOK_DEV))(jax.random.split(key_list[1], device_total)).astype(jnp.int32)
    has_hot = (token_rank < GCAP).astype(jnp.int32)
    other_count = TOPK_GROUP - has_hot
    first_other = jnp.cumsum(other_count, axis=1) - other_count
    other_order = jax.vmap(lambda sub_key: jax.random.permutation(sub_key, N_GROUP - 1))(jax.random.split(key_list[2], device_total)).astype(jnp.int32)
    slot_index = jnp.arange(TOPK_GROUP, dtype=jnp.int32)
    cyclic_pos = (first_other[:, :, None] + slot_index[None, None, :] - has_hot[:, :, None]) % (N_GROUP - 1)
    order_wide = jnp.broadcast_to(other_order[:, None, :], (device_total, TOK_DEV, N_GROUP - 1))
    other_group = jnp.take_along_axis(order_wide, cyclic_pos, axis=2)
    other_group = other_group + (other_group >= hot_group[:, None, None]).astype(jnp.int32)
    first_slot = (has_hot[:, :, None] == 1) & (slot_index[None, None, :] == 0)
    base_groups = jnp.where(first_slot, jnp.broadcast_to(hot_group[:, None, None], other_group.shape), other_group)
    rotation = jax.random.randint(key_list[3], (device_total, TOK_DEV, 1), 0, TOPK_GROUP).astype(jnp.int32)
    groups = jnp.take_along_axis(base_groups, (slot_index[None, None, :] + rotation) % TOPK_GROUP, axis=2)
    candidates = TOPK_GROUP * EPG
    scores = jax.random.randint(key_list[4], (device_total, TOK_DEV, candidates), 0, 1 << 20).astype(jnp.int32) * candidates + jnp.arange(candidates, dtype=jnp.int32)
    chosen = lax.top_k(scores, TOPK)[1].astype(jnp.int32)
    experts = jnp.take_along_axis(groups, chosen // EPG, axis=2) * EPG + chosen % EPG
    return (groups.reshape(TOKENS, TOPK_GROUP), experts.reshape(TOKENS, TOPK))


def draw_picked_group_index(key, part):
    return routing_draws(key)[0]


def draw_picked_expert_index(key, part):
    return routing_draws(key)[1]


def block_scale(rng, extent, shards, smallest, largest):
    loudness = 1.0
    for axis_at, shards_of in shards:
        steps = jax.random.uniform(jax.random.fold_in(jax.random.fold_in(rng, 6), axis_at), (shards_of,), jnp.float32, smallest / len(shards), largest / len(shards))
        loudness = loudness * jnp.repeat(jnp.exp(steps), extent[axis_at] // shards_of).reshape((-1,) + (1,) * (len(extent) - 1 - axis_at))
    return loudness


def normal_values(rng, shape, scale, bound, pieces=(), held_as=jnp.bfloat16):
    factor_of = block_scale(rng, shape, pieces, -0.22, 0.18) if pieces else 1.0
    entries = jax.random.normal(rng, shape, jnp.float32) * scale * factor_of
    return jnp.minimum(jnp.maximum(entries, -bound), bound).astype(held_as)


def setup_inputs(seed: int = 0) -> dict:
    keys = jax.random.split(jax.random.key(seed), 18)
    tokens = normal_values(keys[0], (TOKENS, MODEL_WIDTH), 1.0, 6.0, ((0, 128),))
    picked_group_index = draw_picked_group_index(jax.random.fold_in(keys[17], 71), 0)
    picked_expert_index = draw_picked_expert_index(jax.random.fold_in(keys[17], 71), 0)
    routing_pick_weight = jnp.clip(0.099609375 + 0.49804688 * jax.random.uniform(keys[3], (TOKENS, TOPK), jnp.float32) ** block_scale(keys[3], (TOKENS, TOPK), ((0, 128),), -0.2, 0.2), 0.099609375, 0.59765625).astype(jnp.bfloat16)
    common_gate_weight = normal_values(keys[4], (MODEL_WIDTH, SH_FF), MODEL_WIDTH ** -0.5, 0.0625, ((1, 16),))
    common_up_weight = normal_values(keys[5], (MODEL_WIDTH, SH_FF), MODEL_WIDTH ** -0.5, 0.0625, ((1, 16),))
    common_down_weight = normal_values(keys[6], (SH_FF, MODEL_WIDTH), SH_FF ** -0.5, 0.125, ((0, 16),))
    routed_gate_weight = normal_values(keys[7], (ROUTED_EXPERTS, MODEL_WIDTH, EXPERT_HIDDEN), MODEL_WIDTH ** -0.5, 0.0625, ((0, 8), (2, 16)))
    routed_up_weight = normal_values(keys[8], (ROUTED_EXPERTS, MODEL_WIDTH, EXPERT_HIDDEN), MODEL_WIDTH ** -0.5, 0.0625, ((0, 8), (2, 16)))
    routed_down_weight = normal_values(keys[9], (ROUTED_EXPERTS, EXPERT_HIDDEN, MODEL_WIDTH), EXPERT_HIDDEN ** -0.5, 0.125, ((0, 8), (1, 16)))
    gate_block_scales = jnp.clip(jnp.exp(math.log(2.0) - 1.3862944 * jax.random.uniform(keys[10], (ROUTED_EXPERTS, MODEL_WIDTH // QB, EXPERT_HIDDEN // QB), jnp.float32) ** block_scale(keys[10], (ROUTED_EXPERTS, MODEL_WIDTH // QB, EXPERT_HIDDEN // QB), ((0, 8), (2, 16)), -0.2, 0.2)), 0.5, 2.0)
    up_block_scales = jnp.clip(jnp.exp(math.log(2.0) - 1.3862944 * jax.random.uniform(keys[11], (ROUTED_EXPERTS, MODEL_WIDTH // QB, EXPERT_HIDDEN // QB), jnp.float32) ** block_scale(keys[11], (ROUTED_EXPERTS, MODEL_WIDTH // QB, EXPERT_HIDDEN // QB), ((0, 8), (2, 16)), -0.2, 0.2)), 0.5, 2.0)
    down_block_scales = jnp.clip(jnp.exp(math.log(2.0) - 1.3862944 * jax.random.uniform(keys[12], (ROUTED_EXPERTS, EXPERT_HIDDEN // QB, MODEL_WIDTH // QB), jnp.float32) ** block_scale(keys[12], (ROUTED_EXPERTS, EXPERT_HIDDEN // QB, MODEL_WIDTH // QB), ((0, 8), (1, 16)), -0.2, 0.2)), 0.5, 2.0)
    adapter_input_maps = normal_values(keys[13], (ROUTED_EXPERTS, MODEL_WIDTH, 2 * ADAPTER_RANK), MODEL_WIDTH ** -0.5, 0.0625, ((0, 8),))
    adapter_output_maps = normal_values(keys[14], (ROUTED_EXPERTS, 2, ADAPTER_RANK, EXPERT_HIDDEN), ADAPTER_RANK ** -0.5, 1.5, ((0, 8), (3, 16)))
    adapter_down_input = normal_values(keys[15], (ROUTED_EXPERTS, EXPERT_HIDDEN, ADAPTER_RANK), EXPERT_HIDDEN ** -0.5, 0.125, ((0, 8), (1, 16)))
    adapter_down_output = normal_values(keys[16], (ROUTED_EXPERTS, ADAPTER_RANK, MODEL_WIDTH), ADAPTER_RANK ** -0.5, 1.5, ((0, 8),))
    return {"tokens": tokens, "picked_group_index": picked_group_index, "picked_expert_index": picked_expert_index, "routing_pick_weight": routing_pick_weight, "common_gate_weight": common_gate_weight, "common_up_weight": common_up_weight, "common_down_weight": common_down_weight, "routed_gate_weight": routed_gate_weight, "routed_up_weight": routed_up_weight, "routed_down_weight": routed_down_weight, "gate_block_scales": gate_block_scales, "up_block_scales": up_block_scales, "down_block_scales": down_block_scales, "adapter_input_maps": adapter_input_maps, "adapter_output_maps": adapter_output_maps, "adapter_down_input": adapter_down_input, "adapter_down_output": adapter_down_output}


def dequant(weight, scale):
    expanded = jnp.repeat(jnp.repeat(scale, QB, axis=0), QB, axis=1)
    return (weight.astype(jnp.float32) * expanded).astype(jnp.bfloat16)


def reference(tokens, picked_group_index, picked_expert_index, routing_pick_weight, common_gate_weight, common_up_weight, common_down_weight, routed_gate_weight, routed_up_weight, routed_down_weight, gate_block_scales, up_block_scales, down_block_scales, adapter_input_maps, adapter_output_maps, adapter_down_input, adapter_down_output):
    shared_hidden = (jax.nn.silu(jnp.dot(tokens, common_gate_weight, preferred_element_type=jnp.float32)) * jnp.dot(tokens, common_up_weight, preferred_element_type=jnp.float32)).astype(jnp.bfloat16)
    shared_slice = SH_FF // N_LOCAL
    shared_out = jnp.zeros((TOKENS, MODEL_WIDTH), jnp.float32)
    for block_index in range(N_LOCAL):
        lower_bound = block_index * shared_slice
        shared_part = jnp.dot(shared_hidden[:, lower_bound:lower_bound + shared_slice], common_down_weight[lower_bound:lower_bound + shared_slice], preferred_element_type=jnp.float32).astype(jnp.bfloat16)
        shared_out = shared_out + shared_part.astype(jnp.float32)
    slice_hidden_count = EXPERT_HIDDEN // N_LOCAL
    capacity = N_GROUP * N_LOCAL * GCAP
    expert_numbers = jnp.arange(ROUTED_EXPERTS, dtype=jnp.int32)
    weight_table = jnp.sum(jnp.where(picked_expert_index[:, :, None] == expert_numbers[None, None, :], routing_pick_weight.astype(jnp.float32)[:, :, None], jnp.float32(0.0)), axis=1)
    positions = jnp.arange(TOKENS, dtype=jnp.int32)
    routed = jnp.zeros((TOKENS, MODEL_WIDTH), jnp.float32)
    for group_index in range(N_GROUP):
        chosen = jnp.any(picked_group_index == group_index, axis=1)
        sort_key = jnp.where(chosen, jnp.int32(0), jnp.int32(TOKENS)) + positions
        row_index = jnp.argsort(sort_key)[:capacity].astype(jnp.int32)
        group_token_rows = tokens[row_index]
        partials = [jnp.zeros((capacity, MODEL_WIDTH), jnp.float32) for block_index in range(N_LOCAL)]
        for member in range(EPG):
            current_expert = group_index * EPG + member
            gate_quantized_block = dequant(routed_gate_weight[current_expert], gate_block_scales[current_expert])
            up_quantized_block = dequant(routed_up_weight[current_expert], up_block_scales[current_expert])
            down_quantized_block = dequant(routed_down_weight[current_expert], down_block_scales[current_expert])
            adapter_hidden_rows = jnp.dot(group_token_rows, adapter_input_maps[current_expert], preferred_element_type=jnp.float32).astype(jnp.bfloat16)
            gate_activation = jnp.dot(group_token_rows, gate_quantized_block, preferred_element_type=jnp.float32) + jnp.dot(adapter_hidden_rows[:, :ADAPTER_RANK], adapter_output_maps[current_expert, 0], preferred_element_type=jnp.float32)
            up_activation = jnp.dot(group_token_rows, up_quantized_block, preferred_element_type=jnp.float32) + jnp.dot(adapter_hidden_rows[:, ADAPTER_RANK:], adapter_output_maps[current_expert, 1], preferred_element_type=jnp.float32)
            route_weight = weight_table[row_index, current_expert][:, None]
            hidden_units = (jax.nn.silu(gate_activation) * up_activation * route_weight).astype(jnp.bfloat16)
            for block_index in range(N_LOCAL):
                lower_bound = block_index * slice_hidden_count
                hidden_unit_block = hidden_units[:, lower_bound:lower_bound + slice_hidden_count]
                adapter_down_term = jnp.dot(hidden_unit_block, adapter_down_input[current_expert, lower_bound:lower_bound + slice_hidden_count], preferred_element_type=jnp.float32).astype(jnp.bfloat16)
                summed_terms = jnp.dot(hidden_unit_block, down_quantized_block[lower_bound:lower_bound + slice_hidden_count], preferred_element_type=jnp.float32) + jnp.dot(adapter_down_term, adapter_down_output[current_expert], preferred_element_type=jnp.float32)
                partials[block_index] = partials[block_index] + summed_terms
        group_total = jnp.zeros((capacity, MODEL_WIDTH), jnp.float32)
        for block_index in range(N_LOCAL):
            group_total = group_total + partials[block_index].astype(jnp.bfloat16).astype(jnp.float32)
        group_out = group_total.astype(jnp.bfloat16)
        routed = routed.at[row_index].add(group_out.astype(jnp.float32))
    return (shared_out + routed).astype(jnp.bfloat16)
```

```python
import functools

import jax
import jax.numpy as jnp
from jax import lax
from jax.experimental import pallas as pl
from jax.experimental.pallas import tpu as pltpu
from jax.sharding import PartitionSpec as P

MESH = pl.DeviceIdType.MESH
F32 = jnp.float32
BF16 = jnp.bfloat16

WIDTH = 7168
HALF = WIDTH // 2
SIDE = 4
ROWS = 16
QB = 128
LANES = 128
HID = 384
GU = 2 * HID
DOWN = HID + LANES

UNITS = (
    ((0, 1, 2), 0, 768),
    ((1, 2, 0), 768, 768),
    ((2, 0, 1), 1536, 512),
    ((0, 1, 2), 2048, 512),
    ((1, 2, 0), 2560, 512),
    ((2, 0, 1), 3072, 512),
)
NU = len(UNITS)
PICK_UNIT = 2
EARLY = (0, 1, 2)
LATE = (3, 4, 5)


def gathered_width(u):
    return UNITS[u][2] + (LANES if u == PICK_UNIT else 0)


def cut_of(width):
    return (width // 256) * LANES


def halved(cols, h):
    if h is None:
        return pl.ds(0, cols)
    cut = cut_of(cols)
    return pl.ds(0, cut) if h == 0 else pl.ds(cut, cols - cut)


def slab(order, k, q, own, h, cols):
    ix = [None] * 3
    for j, a in enumerate(order):
        ix[a] = pl.ds(0, SIDE) if j < k else (q if j == k else own[a])
    if k == 0:
        return (*ix, pl.ds(0, ROWS), halved(cols, h))
    if h is not None:
        ix[order[0]] = pl.ds(2 * h, 2)
    return (*ix, pl.ds(0, ROWS), pl.ds(0, cols))


def landing(slot, order, k, h, cols):
    if k == 0:
        return (slot, pl.ds(0, ROWS), halved(cols, h))
    whole = sorted(order[:k])
    ix = [pl.ds(0, SIDE)] * k
    if h is not None:
        ix[whole.index(order[0])] = pl.ds(2 * h, 2)
    return (slot, *ix, pl.ds(0, ROWS), pl.ds(0, cols))


def dot(a, b):
    return jnp.dot(a, b, preferred_element_type=F32)


def dot_t(a, b):
    return lax.dot_general(a, b, (((0,), (0,)), ((), ())), preferred_element_type=F32)


def kernel(*refs):
    it = iter(refs)

    def take(n):
        return [next(it) for _ in range(n)]

    (scales, tokens, picked, weight, out_maps, a_t) = take(6)
    (gate_w, up_w, down_w, sgate_w, sup_w, sdown_w, in_t, b_maps) = take(8)
    (out,) = take(1)
    G = take(NU)
    O = take(NU)
    S = take(NU)
    R = [take(3) for _ in range(NU)]
    (gu, sgu, dcat, in_v, b_v, acc, acc_s, hcat, out_bd, a_bd, xs, xf, fs, fr) = take(14)
    (w_sem, m_sem, x_sem, ag_s, ag_r, as_s, as_r, rs_s, rs_r, ss_s, ss_r) = take(11)

    g = lax.axis_index("group")
    loc = lax.axis_index("local")
    x, c = g // 2, g % 2
    z, y = loc // SIDE, loc % SIDE
    own = (x, y, z)
    o = 1 - c

    def along(axis, step):
        p = (own[axis] + step + SIDE) % SIDE
        if axis == 0:
            return (p * 2 + c, loc)
        if axis == 1:
            return (g, z * SIDE + p)
        return (g, p * SIDE + y)

    sibling = (x * 2 + o, loc)

    def at(axis, step):
        return (own[axis] + step + SIDE) % SIDE

    def remote(src, dst, ss, rs, dev):
        return pltpu.make_async_remote_copy(
            src_ref=src, dst_ref=dst, send_sem=ss, recv_sem=rs, device_id=dev, device_id_type=MESH
        )

    quarter = WIDTH // 4
    mine0 = c * HALF
    other0 = o * HALF
    starts = (mine0, mine0 + quarter, other0, other0 + quarter)

    def w_copy(i, j):
        src = (gate_w if j < 3 else up_w).at[j % 3, pl.ds(starts[i], quarter)]
        return pltpu.make_async_copy(src, gu.at[pl.ds(starts[i], quarter), pl.ds(j * LANES, LANES)], w_sem.at[i, j])

    m_copies = [
        pltpu.make_async_copy(in_t, in_v, m_sem.at[0]),
        pltpu.make_async_copy(sgate_w, sgu.at[:, pl.ds(0, LANES)], m_sem.at[1]),
        pltpu.make_async_copy(sup_w, sgu.at[:, pl.ds(LANES, LANES)], m_sem.at[2]),
        pltpu.make_async_copy(b_maps, b_v, m_sem.at[3]),
        pltpu.make_async_copy(sdown_w, dcat.at[pl.ds(HID, LANES)], m_sem.at[4]),
    ] + [
        pltpu.make_async_copy(down_w.at[e], dcat.at[pl.ds(e * LANES, LANES)], m_sem.at[5 + e]) for e in range(3)
    ]
    m_copies[0].start()
    for i in range(4):
        for j in range(6):
            w_copy(i, j).start()
    for m in m_copies[1:]:
        m.start()

    barrier = pltpu.get_barrier_semaphore()
    partners = [along(a, s) for a in range(3) for s in (1, -1)] + [sibling]
    for p in partners:
        pl.semaphore_signal(barrier, inc=1, device_id=p, device_id_type=MESH)

    lane = lax.broadcasted_iota(jnp.int32, (8, LANES), 1)
    pick = jnp.zeros((8, LANES), F32)
    for k in range(8):
        pick = pick + jnp.where(lane == picked[:, k : k + 1], weight[:, k : k + 1].astype(F32), 0.0)
    xs[:, pl.ds(0, HALF)] = tokens[:, pl.ds(pl.multiple_of(other0, LANES), HALF)].astype(F32)
    xs[:, pl.ds(HALF, LANES)] = pick
    xf[c, :, pl.ds(0, HALF)] = tokens[:, pl.ds(pl.multiple_of(mine0, LANES), HALF)].astype(F32)
    xf[c, :, pl.ds(HALF, LANES)] = pick
    pl.semaphore_wait(barrier, len(partners))
    swap = remote(xs, xf.at[c], x_sem.at[0], x_sem.at[1], sibling)
    swap.start()

    out_bd[...] = jnp.zeros_like(out_bd)
    a_bd[...] = jnp.zeros_like(a_bd)
    for e in range(3):
        for h in range(2):
            out_bd[pl.ds(e * 32 + h * 16, 16), pl.ds((h * 3 + e) * LANES, LANES)] = out_maps[e, h]
        a_bd[pl.ds(e * 16, 16), pl.ds(e * LANES, LANES)] = a_t[e]
    hcat[:, :, :, :, pl.ds(HID, LANES)] = jnp.zeros((SIDE, SIDE, SIDE, ROWS, LANES), BF16)

    swap.wait_send()
    remote(xs, xf.at[o], x_sem.at[0], x_sem.at[1], sibling).wait_recv()
    block = xf[...].reshape(ROWS, HALF + LANES).astype(BF16)
    for u, (order, first, cols) in enumerate(UNITS):
        G[u][x, y, z, :, pl.ds(0, cols)] = block[:, first : first + cols]
        if u == PICK_UNIT:
            G[u][x, y, z, :, pl.ds(cols, LANES)] = block[:, HALF:]

    def ag(u, k, which, arriving=False):
        order = UNITS[u][0]
        a = order[k]
        w = gathered_width(u)
        step = 1 if which in (0, 2) else -1
        if which < 2:
            sent, got, h = at(a, 0), at(a, -step), None
        else:
            sent, got, h = at(a, -step), at(a, -2 * step), which - 2
        part = G[u].at[slab(order, k, got if arriving else sent, own, h, w)]
        return remote(part, part, ag_s.at[u, k, which], ag_r.at[u, k, which], along(a, step))

    def ag_open(u, k):
        for which in (0, 1):
            ag(u, k, which).start()

    def ag_forward(u, k):
        for which in (0, 1):
            ag(u, k, which, True).wait_recv()
            ag(u, k, which + 2).start()

    def ag_close(u, k):
        for which in (2, 3):
            ag(u, k, which, True).wait_recv()

    QUARTER = (0, -1, 1, 2)

    def hand(u, i):
        order, _, cols = UNITS[u]
        at_q = slab(order, 2, at(order[2], QUARTER[i]), own, None, cols)
        return remote(G[u].at[at_q], O[u].at[at_q], as_s.at[u, i], as_r.at[u, i], sibling)

    def gate_up(u, i, src, first0):
        order, first, cols = UNITS[u]
        at_q = slab(order, 2, at(order[2], QUARTER[i]), own, None, cols)
        at_a = slab(order, 2, at(order[2], QUARTER[i]), own, None, GU)
        rows = pl.ds(pl.multiple_of(first0 + first, LANES), cols)
        got = dot(src[at_q].reshape(256, cols), gu[rows, :]).reshape(SIDE, SIDE, ROWS, GU)
        acc[at_a] = acc[at_a] + got

    def shared(u, src, first0):
        _, first, cols = UNITS[u]
        rows = pl.ds(pl.multiple_of(first0 + first, LANES), cols)
        acc_s[...] += dot(src[x, pl.ds(2 * c, 2), :, :, pl.ds(0, cols)].reshape(128, cols), sgu[rows, :])

    def merge_up(k0, n):
        def body(i, carry):
            kb = k0 + i
            ks = pl.ds(pl.multiple_of(kb * QB, QB), QB)
            ab = dot_t(in_v[:, :, ks].reshape(96, QB), out_bd[...])
            for j in range(6):
                cs = pl.ds(j * LANES, LANES)
                s = scales[j * 56 + kb]
                gu[ks, cs] = (gu[ks, cs].astype(F32) * s + ab[:, j * LANES : (j + 1) * LANES]).astype(BF16)
            return carry

        lax.fori_loop(0, n, body, 0)

    def merge_down():
        def body(i, carry):
            ns = pl.ds(pl.multiple_of(i * 256, 256), 256)
            ab = dot_t(a_bd[...], b_v[:, :, ns].reshape(48, 256))
            for e in range(3):
                for t in range(2):
                    at_d = (pl.ds(e * LANES, LANES), pl.ds(pl.multiple_of(i * 256 + t * 128, 128), 128))
                    s = scales[336 + e * 56 + i * 2 + t]
                    part = ab[e * 128 : (e + 1) * 128, t * 128 : (t + 1) * 128]
                    dcat[at_d] = (dcat[at_d].astype(F32) * s + part).astype(BF16)
            return carry

        lax.fori_loop(0, WIDTH // 256, body, 0)

    def wait_w(i):
        for j in range(6):
            w_copy(i, j).wait()

    ALL = EARLY + LATE
    for u in ALL:
        ag_open(u, 0)
    acc[...] = jnp.zeros_like(acc)
    acc_s[...] = jnp.zeros_like(acc_s)
    m_copies[0].wait()
    wait_w(0)
    for u in ALL:
        ag_forward(u, 0)
    merge_up(c * 28, 7)
    for u in ALL:
        ag_close(u, 0)
        ag_open(u, 1)
    merge_up(c * 28 + 7, 7)
    wait_w(1)
    for u in ALL:
        ag_forward(u, 1)
    merge_up(c * 28 + 14, 14)
    for u in ALL:
        ag_close(u, 1)
        ag_open(u, 2)
        hand(u, 0).start()
    for u in EARLY:
        gate_up(u, 0, G[u], mine0)
    wait_w(2)
    wait_w(3)
    merge_up(o * 28, 28)
    for u in EARLY:
        hand(u, 0).wait_recv()
        gate_up(u, 0, O[u], other0)
    for u in EARLY:
        ag_forward(u, 2)
        hand(u, 1).start()
        hand(u, 2).start()
    for u in LATE:
        gate_up(u, 0, G[u], mine0)
        hand(u, 0).wait_recv()
        gate_up(u, 0, O[u], other0)
    for u in EARLY:
        gate_up(u, 1, G[u], mine0)
        gate_up(u, 2, G[u], mine0)
        hand(u, 1).wait_recv()
        gate_up(u, 1, O[u], other0)
        hand(u, 2).wait_recv()
        gate_up(u, 2, O[u], other0)
    for u in LATE:
        ag_forward(u, 2)
        hand(u, 1).start()
        hand(u, 2).start()
    for m in m_copies[1:]:
        m.wait()
    merge_down()
    for u in EARLY:
        ag_close(u, 2)
        hand(u, 3).start()
    for u in LATE:
        gate_up(u, 1, G[u], mine0)
        gate_up(u, 2, G[u], mine0)
        hand(u, 1).wait_recv()
        gate_up(u, 1, O[u], other0)
        hand(u, 2).wait_recv()
        gate_up(u, 2, O[u], other0)
    for u in EARLY:
        gate_up(u, 3, G[u], mine0)
        shared(u, G[u], mine0)
        hand(u, 3).wait_recv()
        gate_up(u, 3, O[u], other0)
        shared(u, O[u], other0)
    for u in LATE:
        ag_close(u, 2)
        hand(u, 3).start()
    for u in LATE:
        gate_up(u, 3, G[u], mine0)
        shared(u, G[u], mine0)
    for u in LATE:
        hand(u, 3).wait_recv()
        gate_up(u, 3, O[u], other0)
        shared(u, O[u], other0)

    choose = (
        lax.broadcasted_iota(jnp.int32, (LANES, HID), 0)
        == lax.broadcasted_iota(jnp.int32, (LANES, HID), 1) // LANES + g * 3
    ).astype(BF16)
    pick_cols = pl.ds(UNITS[PICK_UNIT][2], LANES)

    def activate(i, carry):
        xi, yi = i // SIDE, i % SIDE
        gate = acc[xi, yi, :, :, pl.ds(0, HID)].reshape(64, HID)
        up = acc[xi, yi, :, :, pl.ds(HID, HID)].reshape(64, HID)
        picks = dot(G[PICK_UNIT][xi, yi, :, :, pick_cols].reshape(64, LANES), choose)
        hidden = (gate / (1.0 + jnp.exp(-gate)) * up * picks).astype(BF16)
        hcat[xi, yi, :, :, pl.ds(0, HID)] = hidden.reshape(SIDE, ROWS, HID)
        return carry

    lax.fori_loop(0, SIDE * SIDE, activate, 0)
    sg = acc_s[:, pl.ds(0, LANES)]
    su = acc_s[:, pl.ds(LANES, LANES)]
    hcat[x, pl.ds(2 * c, 2), :, :, pl.ds(HID, LANES)] = (
        (sg / (1.0 + jnp.exp(-sg)) * su).astype(BF16).reshape(2, SIDE, ROWS, LANES)
    )

    for u in ALL:
        for k in range(3):
            for which in range(4):
                ag(u, k, which).wait_send()
        for i in range(4):
            hand(u, i).wait_send()

    def rows_of(u, i):
        order = UNITS[u][0]
        at_h = slab(order, 2, at(order[2], QUARTER[i]), own, None, DOWN)
        return hcat[at_h].reshape(256, DOWN)

    def give(u, i):
        order, _, cols = UNITS[u]
        at_q = slab(order, 2, at(order[2], QUARTER[i]), own, None, cols)
        return remote(O[u].at[at_q], S[u].at[at_q], ss_s.at[u, i], ss_r.at[u, i], sibling)

    def down_other(u, i):
        order, first, cols = UNITS[u]
        at_q = slab(order, 2, at(order[2], QUARTER[i]), own, None, cols)
        ns = pl.ds(pl.multiple_of(other0 + first, LANES), cols)
        O[u][at_q] = dot(rows_of(u, i), dcat[:, ns]).astype(BF16).reshape(SIDE, SIDE, ROWS, cols)
        give(u, i).start()

    def down_mine(u, i):
        order, first, cols = UNITS[u]
        at_q = slab(order, 2, at(order[2], QUARTER[i]), own, None, cols)
        ns = pl.ds(pl.multiple_of(mine0 + first, LANES), cols)
        mine = dot(rows_of(u, i), dcat[:, ns]).reshape(SIDE, SIDE, ROWS, cols)
        give(u, i).wait_recv()
        G[u][at_q] = (mine + S[u][at_q].astype(F32)).astype(BF16)

    def rs(u, k, which):
        order, _, cols = UNITS[u]
        a = order[k]
        right = which % 2 == 0
        step = 1 if right else -1
        if which < 2:
            q, h, slot = at(a, 2), which, 0
        elif which < 4:
            q, h, slot = at(a, step), (1 if right else 0), (1 if right else 2)
        else:
            q, h, slot = at(a, step), (0 if right else 1), (1 if right else 2)
        src = G[u].at[slab(order, k, q, own, h, cols)]
        dst = R[u][k].at[landing(slot, order, k, h, cols)]
        return remote(src, dst, rs_s.at[u, k, which], rs_r.at[u, k, which], along(a, step))

    def rs_far(u, k):
        rs(u, k, 0).start()
        rs(u, k, 1).start()

    def rs_near(u, k, which):
        rs(u, k, which).start()

    def rs_pass(u, k):
        order, _, cols = UNITS[u]
        a = order[k]
        for which in (0, 1):
            step = 1 if which == 0 else -1
            rs(u, k, which).wait_recv()
            at_q = slab(order, k, at(a, step), own, which, cols)
            came = R[u][k][landing(0, order, k, which, cols)]
            G[u][at_q] = (G[u][at_q].astype(F32) + came.astype(F32)).astype(BF16)
            rs(u, k, 4 + which).start()

    def rs_sum(u, k):
        order, _, cols = UNITS[u]
        for which in (2, 3, 4, 5):
            rs(u, k, which).wait_recv()
        at_q = slab(order, k, own[order[k]], own, None, cols)
        l = R[u][k][landing(1, order, k, None, cols)]
        r = R[u][k][landing(2, order, k, None, cols)]
        return at_q, G[u][at_q].astype(F32) + (l.astype(F32) + r.astype(F32))

    def rs_next(u, k):
        at_q, total = rs_sum(u, k)
        G[u][at_q] = total.astype(BF16)
        rs_far(u, k - 1)
        rs_near(u, k - 1, 2)
        rs_near(u, k - 1, 3)

    def first_half(us):
        for u in us:
            down_other(u, 3)
        for u in us:
            down_other(u, 2)
        for u in us:
            down_mine(u, 3)
            rs_far(u, 2)
        for u in us:
            down_other(u, 1)
        for u in us:
            down_mine(u, 2)
            rs_near(u, 2, 2)
        for u in us:
            down_mine(u, 1)
            rs_near(u, 2, 3)

    first_half(EARLY)
    for u in EARLY:
        down_other(u, 0)
    first_half(LATE)
    for u in EARLY:
        rs_pass(u, 2)
    for u in LATE:
        down_other(u, 0)
    for u in EARLY:
        down_mine(u, 0)
    for u in LATE:
        rs_pass(u, 2)
    for u in LATE:
        down_mine(u, 0)
    for us in (EARLY, LATE):
        for u in us:
            rs_next(u, 2)
    for us in (EARLY, LATE):
        for u in us:
            rs_pass(u, 1)
    for us in (EARLY, LATE):
        for u in us:
            rs_next(u, 1)
    for us in (EARLY, LATE):
        for u in us:
            rs_pass(u, 0)
    for us in (EARLY, LATE):
        for u in us:
            _, first, cols = UNITS[u]
            _, total = rs_sum(u, 0)
            fs[:, :, pl.ds(first, cols)] = total.reshape(2, 8, cols)

    final = remote(fs.at[o], fr, x_sem.at[2], x_sem.at[3], sibling)
    final.start()
    out[:, pl.ds(pl.multiple_of(mine0, LANES), HALF)] = fs[c].astype(BF16)
    final.wait_recv()
    out[:, pl.ds(pl.multiple_of(other0, LANES), HALF)] = fr[...].astype(BF16)
    final.wait_send()
    for u in ALL:
        for k in range(3):
            for which in range(6):
                rs(u, k, which).wait_send()
        for i in range(4):
            give(u, i).wait_send()


def on_device(
    tokens,
    picked_group_index,
    picked_expert_index,
    routing_pick_weight,
    common_gate_weight,
    common_up_weight,
    common_down_weight,
    routed_gate_weight,
    routed_up_weight,
    routed_down_weight,
    gate_block_scales,
    up_block_scales,
    down_block_scales,
    adapter_input_maps,
    adapter_output_maps,
    adapter_down_input,
    adapter_down_output,
):
    scales = jnp.concatenate(
        [gate_block_scales.reshape(-1), up_block_scales.reshape(-1), down_block_scales.reshape(-1)]
    )
    vmem = pl.BlockSpec(memory_space=pltpu.VMEM)
    hbm = pl.BlockSpec(memory_space=pl.ANY)
    scratch = []
    for u, (_, _, cols) in enumerate(UNITS):
        scratch.append(pltpu.VMEM((SIDE, SIDE, SIDE, ROWS, gathered_width(u)), BF16))
    for _ in range(2):
        for _, _, cols in UNITS:
            scratch.append(pltpu.VMEM((SIDE, SIDE, SIDE, ROWS, cols), BF16))
    for _, _, cols in UNITS:
        for k in range(3):
            scratch.append(pltpu.VMEM((3, *([SIDE] * k), ROWS, cols), BF16))
    scratch += [
        pltpu.VMEM((WIDTH, GU), BF16),
        pltpu.VMEM((WIDTH, 2 * LANES), BF16),
        pltpu.VMEM((DOWN, WIDTH), BF16),
        pltpu.VMEM((3, 32, WIDTH), BF16),
        pltpu.VMEM((3, 16, WIDTH), BF16),
        pltpu.VMEM((SIDE, SIDE, SIDE, ROWS, GU), F32),
        pltpu.VMEM((128, 2 * LANES), F32),
        pltpu.VMEM((SIDE, SIDE, SIDE, ROWS, DOWN), BF16),
        pltpu.VMEM((96, GU), BF16),
        pltpu.VMEM((48, HID), BF16),
        pltpu.VMEM((8, HALF + LANES), F32),
        pltpu.VMEM((2, 8, HALF + LANES), F32),
        pltpu.VMEM((2, 8, HALF), F32),
        pltpu.VMEM((8, HALF), F32),
        pltpu.SemaphoreType.DMA((4, 6)),
        pltpu.SemaphoreType.DMA((8,)),
        pltpu.SemaphoreType.DMA((4,)),
        pltpu.SemaphoreType.DMA((NU, 3, 4)),
        pltpu.SemaphoreType.DMA((NU, 3, 4)),
        pltpu.SemaphoreType.DMA((NU, 4)),
        pltpu.SemaphoreType.DMA((NU, 4)),
        pltpu.SemaphoreType.DMA((NU, 3, 6)),
        pltpu.SemaphoreType.DMA((NU, 3, 6)),
        pltpu.SemaphoreType.DMA((NU, 4)),
        pltpu.SemaphoreType.DMA((NU, 4)),
    ]
    return pl.pallas_call(
        kernel,
        out_shape=jax.ShapeDtypeStruct((8, WIDTH), BF16),
        in_specs=[pl.BlockSpec(memory_space=pltpu.SMEM)] + [vmem] * 5 + [hbm] * 8,
        out_specs=vmem,
        scratch_shapes=scratch,
        compiler_params=pltpu.CompilerParams(
            collective_id=0, has_side_effects=True, vmem_limit_bytes=62 * 2**20
        ),
        cost_estimate=pl.CostEstimate(flops=22 * 10**9, bytes_accessed=25 * 10**6, transcendentals=10**6),
    )(
        scales,
        tokens,
        picked_expert_index,
        routing_pick_weight,
        adapter_output_maps,
        adapter_down_input.transpose(0, 2, 1),
        routed_gate_weight,
        routed_up_weight,
        routed_down_weight,
        common_gate_weight,
        common_up_weight,
        common_down_weight,
        adapter_input_maps.transpose(0, 2, 1),
        adapter_down_output,
    )


def solution(mesh):
    in_specs = (
        P(("group", "local"), None),
        P(("group", "local"), None),
        P(("group", "local"), None),
        P(("group", "local"), None),
        P(None, "local"),
        P(None, "local"),
        P("local", None),
        P("group", None, "local"),
        P("group", None, "local"),
        P("group", "local", None),
        P("group", None, "local"),
        P("group", None, "local"),
        P("group", "local", None),
        P("group", None, None),
        P("group", None, None, "local"),
        P("group", "local", None),
        P("group", None, None),
    )
    return jax.shard_map(
        on_device, mesh=mesh, in_specs=in_specs, out_specs=P(("group", "local"), None), check_vma=False
    )
```

```python
import functools

import jax
import jax.numpy as jnp
from jax import lax
from jax.experimental import pallas as pl
from jax.experimental.pallas import tpu as pltpu
from jax.sharding import PartitionSpec as P

MESH = pl.DeviceIdType.MESH
F32 = jnp.float32
BF16 = jnp.bfloat16

WIDTH = 7168
HALF = WIDTH // 2
SIDE = 4
ROWS = 16
QB = 128
LANES = 128
HID = 384
GU = 2 * HID
DOWN = HID + LANES

UNITS = (
    ((0, 1, 2), 0, 1280),
    ((1, 2, 0), 1280, 1280),
    ((2, 0, 1), 2560, 1024),
)
NU = len(UNITS)
PICK_UNIT = 2
REL = (0, 1, -1, 2)

AG_GROUPS = (
    ((0, 0, 0),),
    ((0, 0, 1),),
    ((0, 0, 2), (0, 1, 2)),
    ((1, 0, 0), (1, -1, 1)),
    ((1, 1, 0), (1, 2, 1)),
    ((1, -1, 0), (1, 2, 0)),
    ((1, 0, 1), (1, 1, 1)),
    ((1, 0, 2), (1, 1, 2), (1, -1, 2), (1, 2, 2)),
    ((2, 0, 0), (2, 0, 1)),
    ((2, -1, 0), (2, -1, 1)),
    ((2, 1, 0), (2, 1, 1)),
    ((2, 2, 0), (2, 2, 1)),
    ((2, 0, 2), (2, -1, 2)),
    ((2, 1, 2), (2, 2, 2)),
)
AG_WAITS = len(AG_GROUPS)
AG_GROUP_OF = {copy: i for i, group in enumerate(AG_GROUPS) for copy in group}
HERE = ((None, 0),)
NEAR_A = ((0, -1), (0, 1), (-1, -1), (-1, 1))
NEAR_B = ((1, -1), (1, 1), (2, -1), (2, 1))
FAR_A = ((0, 2), (-1, 2))
FAR_B = ((1, 2), (2, 2))
HAND_GROUPS = (HERE, NEAR_A, NEAR_B, FAR_A, FAR_B)


def gathered_width(u):
    return UNITS[u][2] + (LANES if u == PICK_UNIT else 0)


def halved(cols, h):
    if h is None:
        return pl.ds(0, cols)
    cut = cols // 256 * LANES
    return pl.ds(0, cut) if h == 0 else pl.ds(cut, cols - cut)


def landing(slot, order, k, piece, at, cols):
    if k == 0:
        return (slot, pl.ds(0, ROWS), halved(cols, piece))
    whole = sorted(order[:k])
    ix = [pl.ds(0, SIDE)] * k
    if piece is not None:
        ix[whole.index(order[k - 1])] = at(order[k - 1], piece)
    return (slot, *ix, pl.ds(0, ROWS), pl.ds(0, cols))


def dot(a, b):
    return jnp.dot(a, b, preferred_element_type=F32)


def dot_t(a, b):
    return lax.dot_general(a, b, (((0,), (0,)), ((), ())), preferred_element_type=F32)


def kernel(*refs):
    it = iter(refs)

    def take(n):
        return [next(it) for _ in range(n)]

    small_in = take(8)
    (gate_w, up_w, down_w, sgate_w, sup_w, sdown_w, in_t, b_maps) = take(8)
    (out,) = take(1)
    G = take(NU)
    O = take(NU)
    S = take(NU)
    R = [take(3) for _ in range(NU)]
    (gu, sgu, dcat, in_v, b_v, acc, acc_s, hcat, out_bd, a_bd, xs, xf, fs, fr) = take(14)
    small = take(8)
    (gate_s, up_s, down_s, tokens, picked, weight, out_maps, a_t) = small
    (i_sem, w_sem, m_sem, x_sem, ag_s, ag_r, as_s, as_r, rs_s, rs_r, ss_s, ss_r) = take(12)

    g = lax.axis_index("group")
    loc = lax.axis_index("local")
    x, c = g // 2, g % 2
    z, y = loc // SIDE, loc % SIDE
    own = (x, y, z)
    o = 1 - c

    def along(axis, step):
        p = (own[axis] + step + SIDE) % SIDE
        if axis == 0:
            return (p * 2 + c, loc)
        if axis == 1:
            return (g, z * SIDE + p)
        return (g, p * SIDE + y)

    sibling = (x * 2 + o, loc)

    def at(axis, step):
        return (own[axis] + step + SIDE) % SIDE

    def part(order, k, q, piece, cols):
        ix = list(own)
        for a in order[:k]:
            ix[a] = pl.ds(0, SIDE)
        ix[order[k]] = at(order[k], q)
        if k == 0:
            return (*ix, pl.ds(0, ROWS), halved(cols, piece))
        if piece is not None:
            ix[order[k - 1]] = at(order[k - 1], piece)
        return (*ix, pl.ds(0, ROWS), pl.ds(0, cols))

    def remote(src, dst, ss, rs, dev):
        return pltpu.make_async_remote_copy(
            src_ref=src, dst_ref=dst, send_sem=ss, recv_sem=rs, device_id=dev, device_id_type=MESH
        )

    barrier = pltpu.get_barrier_semaphore()
    partners = [along(a, s) for a in range(3) for s in (1, -1)] + [sibling]
    for p in partners:
        pl.semaphore_signal(barrier, inc=1, device_id=p, device_id_type=MESH)

    inward = [pltpu.make_async_copy(a, b, i_sem.at[i]) for i, (a, b) in enumerate(zip(small_in, small))]
    for i in (3, 4, 5, 6, 7, 0, 1, 2):
        inward[i].start()
    mine0 = c * HALF
    other0 = o * HALF
    w_rows = ((mine0, HALF // 2), (mine0 + HALF // 2, HALF // 2), (other0, HALF))

    def w_copy(i, j):
        rows = pl.ds(*w_rows[i])
        src = (gate_w if j < 3 else up_w).at[j % 3, rows]
        return pltpu.make_async_copy(src, gu.at[rows, pl.ds(j * LANES, LANES)], w_sem.at[i])

    def m_copy(i):
        if i == 0:
            return pltpu.make_async_copy(in_t, in_v, m_sem.at[0])
        if i < 3:
            src = sgate_w if i == 1 else sup_w
            return pltpu.make_async_copy(src, sgu.at[:, pl.ds((i - 1) * LANES, LANES)], m_sem.at[1])
        if i == 3:
            return pltpu.make_async_copy(b_maps, b_v, m_sem.at[2])
        if i == 4:
            return pltpu.make_async_copy(sdown_w, dcat.at[pl.ds(HID, LANES)], m_sem.at[3])
        return pltpu.make_async_copy(down_w.at[i - 5], dcat.at[pl.ds((i - 5) * LANES, LANES)], m_sem.at[3])

    def wait_all(ref, sem):
        pltpu.make_async_copy(ref, ref, sem).wait()

    m_copy(0).start()
    for j in range(6):
        w_copy(0, j).start()

    out_bd[...] = jnp.zeros_like(out_bd)
    a_bd[...] = jnp.zeros_like(a_bd)
    hcat[:, :, :, :, pl.ds(HID, LANES)] = jnp.zeros((SIDE, SIDE, SIDE, ROWS, LANES), BF16)
    for i in (3, 4, 5):
        inward[i].wait()
    lane = lax.broadcasted_iota(jnp.int32, (8, LANES), 1)
    pick = jnp.zeros((8, LANES), F32)
    for k in range(8):
        pick = pick + jnp.where(lane == picked[:, k : k + 1], weight[:, k : k + 1].astype(F32), 0.0)
    xs[:, pl.ds(0, HALF)] = tokens[:, pl.ds(pl.multiple_of(other0, LANES), HALF)].astype(F32)
    xs[:, pl.ds(HALF, LANES)] = pick
    xf[c, :, pl.ds(0, HALF)] = tokens[:, pl.ds(pl.multiple_of(mine0, LANES), HALF)].astype(F32)
    xf[c, :, pl.ds(HALF, LANES)] = pick
    pl.semaphore_wait(barrier, len(partners))
    swap = remote(xs, xf.at[c], x_sem.at[0], x_sem.at[1], sibling)
    swap.start()

    for i in (1, 2):
        for j in range(6):
            w_copy(i, j).start()
    for i in range(1, 8):
        m_copy(i).start()
    for i in (6, 7, 0, 1, 2):
        inward[i].wait()
    for e in range(3):
        for h in range(2):
            out_bd[pl.ds(e * 32 + h * 16, 16), pl.ds((h * 3 + e) * LANES, LANES)] = out_maps[e, h]
        a_bd[pl.ds(e * 16, 16), pl.ds(e * LANES, LANES)] = a_t[e]
    swap.wait_send()
    remote(xs, xf.at[o], x_sem.at[0], x_sem.at[1], sibling).wait_recv()
    block = xf[...].reshape(ROWS, HALF + LANES).astype(BF16)
    for u, (order, first, cols) in enumerate(UNITS):
        G[u][x, y, z, :, pl.ds(0, cols)] = block[:, first : first + cols]
        if u == PICK_UNIT:
            G[u][x, y, z, :, pl.ds(cols, LANES)] = block[:, HALF:]

    def ag(u, k, piece, kind, arriving=False):
        order = UNITS[u][0]
        if kind == 2:
            step = 1 if piece in ((0,) if k == 0 else (0, 1)) else -1
            q = -2 * step if arriving else -step
        else:
            step = 1 if kind == 0 else -1
            q = -step if arriving else 0
        which = None if k == 0 and kind < 2 else piece
        block = G[u].at[part(order, k, q, which, gathered_width(u))]
        sem = AG_GROUP_OF[(k, piece, kind)]
        return remote(block, block, ag_s.at[u, k], ag_r.at[u, sem], along(order[k], step))

    def ag_send(u, k, piece):
        ag(u, k, piece, 0).start()
        ag(u, k, piece, 1).start()

    def blocks_of(ref, k, n, cols):
        ix = [0, 0, 0, pl.ds(0, ROWS), pl.ds(0, cols)]
        if k > 0:
            ix[3 - k] = pl.ds(0, n)
            for j in range(4 - k, 3):
                ix[j] = pl.ds(0, SIDE)
        return ref.at[tuple(ix)]

    def ag_got(u, i):
        k, _, kind = AG_GROUPS[i][0]
        n = len(AG_GROUPS[i])
        if k == 0:
            n = 1
        ref = blocks_of(G[u], max(k, 1), n, gathered_width(u))
        remote(ref, ref, ag_s.at[u, k], ag_r.at[u, i], sibling).wait_recv()

    def ag_pass(u, k, piece):
        ag(u, k, piece, 2).start()

    def ag_left(u, k):
        ref = blocks_of(G[u], k + 1, 3, gathered_width(u))
        remote(ref, ref, ag_s.at[u, k], ag_r.at[u, 0], sibling).wait_send()

    def line_a(u):
        ag_got(u, 0)
        ag_pass(u, 0, 0)
        ag_send(u, 1, -1)
        ag_got(u, 1)
        ag_pass(u, 0, 1)
        ag_send(u, 1, 1)

    def line_b(u):
        ag_got(u, 2)
        ag_send(u, 1, 2)
        ag_send(u, 2, 0)

    def plane_a(u):
        ag_got(u, 3)
        ag_pass(u, 1, 0)
        ag_pass(u, 1, -1)
        ag_got(u, 4)
        ag_pass(u, 1, 1)
        ag_pass(u, 1, 2)

    def plane_b(u):
        ag_got(u, 5)
        ag_send(u, 2, -1)
        ag_got(u, 6)
        ag_send(u, 2, 1)

    def plane_c(u):
        ag_got(u, 7)
        ag_send(u, 2, 2)
        hand(u, None, 0).start()

    def cube_a(u, piece):
        ag_got(u, {0: 8, -1: 9, 1: 10, 2: 11}[piece])
        ag_pass(u, 2, piece)
        hand(u, piece, -1).start()
        hand(u, piece, 1).start()

    def cube_b(u, i):
        ag_got(u, 12 + i)
        for r, q in (FAR_A, FAR_B)[i]:
            hand(u, r, q).start()

    def hand(u, piece, q):
        order, _, cols = UNITS[u]
        block = part(order, 2, q, piece, cols)
        (i,) = (i for i, rows in enumerate(HAND_GROUPS) if (piece, q) in rows)
        return remote(G[u].at[block], O[u].at[block], as_s.at[u], as_r.at[u, i], sibling)

    def gate_up(u, src, first0, rows):
        order, first, cols = UNITS[u]
        ws = pl.ds(pl.multiple_of(first0 + first, LANES), cols)
        if len(rows) == 1:
            lhs = src[part(order, 2, rows[0][1], None, cols)].reshape(256, cols)
            at_a = part(order, 2, rows[0][1], None, GU)
            acc[at_a] = acc[at_a] + dot(lhs, gu[ws, :]).reshape(SIDE, SIDE, ROWS, GU)
            return
        lhs = jnp.concatenate([src[part(order, 2, q, r, cols)].reshape(64, cols) for r, q in rows], axis=0)
        got = dot(lhs, gu[ws, :])
        for i, (r, q) in enumerate(rows):
            at_a = part(order, 2, q, r, GU)
            acc[at_a] = acc[at_a] + got[i * 64 : (i + 1) * 64].reshape(SIDE, ROWS, GU)

    def from_sibling(u, rows):
        n = SIDE if rows is HERE else len(rows)
        ref = blocks_of(O[u], 2, n, UNITS[u][2])
        remote(ref, ref, as_s.at[u], as_r.at[u, HAND_GROUPS.index(rows)], sibling).wait_recv()
        gate_up(u, O[u], other0, rows)

    def shared(u, src, first0):
        _, first, cols = UNITS[u]
        ws = pl.ds(pl.multiple_of(first0 + first, LANES), cols)
        acc_s[...] += dot(src[x, pl.ds(2 * c, 2), :, :, pl.ds(0, cols)].reshape(128, cols), sgu[ws, :])

    def merge_up(first, n):
        def body(i, carry):
            kb = first + i * 4
            ab = dot_t(in_v[:, :, pl.ds(pl.multiple_of(kb * QB, QB), 4 * QB)].reshape(96, 4 * QB), out_bd[...])
            for t in range(4):
                ks = pl.ds(pl.multiple_of(kb * QB, QB) + t * QB, QB)
                for j in range(6):
                    cs = pl.ds(j * LANES, LANES)
                    s = (gate_s if j < 3 else up_s)[j % 3, 0, kb + t]
                    add = ab[t * QB : (t + 1) * QB, j * LANES : (j + 1) * LANES]
                    gu[ks, cs] = (gu[ks, cs].astype(F32) * s + add).astype(BF16)
            return carry

        lax.fori_loop(0, n, body, 0)

    def merge_down(first, n):
        def body(i, carry):
            n0 = pl.multiple_of((first + i) * 1024, 1024)
            ab = dot_t(a_bd[...], b_v[:, :, pl.ds(n0, 1024)].reshape(48, 1024))
            for e in range(3):
                for t in range(8):
                    at_d = (pl.ds(e * LANES, LANES), pl.ds(n0 + t * QB, QB))
                    s = down_s[e, 0, (first + i) * 8 + t]
                    add = ab[e * LANES : (e + 1) * LANES, t * QB : (t + 1) * QB]
                    dcat[at_d] = (dcat[at_d].astype(F32) * s + add).astype(BF16)
            return carry

        lax.fori_loop(0, n, body, 0)

    def wait_w(i):
        wait_all(gu.at[pl.ds(*w_rows[i])], w_sem.at[i])

    ALL = range(NU)
    for u in ALL:
        ag_send(u, 0, 0)
    for u in ALL:
        ag_send(u, 1, 0)
    acc[...] = jnp.zeros_like(acc)
    acc_s[...] = jnp.zeros_like(acc_s)
    m_copy(0).wait()
    wait_w(0)
    merge_up(c * 28, 2)
    for u in ALL:
        line_a(u)
    merge_up(c * 28 + 8, 1)
    wait_w(1)
    merge_up(c * 28 + 12, 2)
    for u in ALL:
        line_b(u)
    merge_up(c * 28 + 20, 2)
    for u in ALL:
        plane_a(u)
    wait_w(2)
    merge_up(o * 28, 2)
    for u in ALL:
        plane_b(u)
    merge_up(o * 28 + 8, 2)
    for u in ALL:
        plane_c(u)
    merge_up(o * 28 + 16, 3)
    for u in ALL:
        gate_up(u, G[u], mine0, HERE)
    for u in ALL:
        cube_a(u, 0)
    for u in ALL:
        from_sibling(u, HERE)
    m_copy(3).wait()
    wait_all(dcat, m_sem.at[3])
    merge_down(0, 3)
    for u in ALL:
        cube_a(u, -1)
    for u in ALL:
        gate_up(u, G[u], mine0, NEAR_A)
    merge_down(3, 4)
    for u in ALL:
        cube_a(u, 1)
    for u in ALL:
        from_sibling(u, NEAR_A)
    for u in ALL:
        cube_a(u, 2)
    for u in ALL:
        gate_up(u, G[u], mine0, NEAR_B)
    for u in ALL:
        from_sibling(u, NEAR_B)
    wait_all(sgu, m_sem.at[1])
    for u in ALL:
        cube_b(u, 0)
    for u in ALL:
        gate_up(u, G[u], mine0, FAR_A)
    for u in ALL:
        from_sibling(u, FAR_A)
    for u in ALL:
        for k in (0, 1):
            ag_left(u, k)
    for u in ALL:
        cube_b(u, 1)
    for u in ALL:
        gate_up(u, G[u], mine0, FAR_B)
        shared(u, G[u], mine0)
    for u in ALL:
        from_sibling(u, FAR_B)
        shared(u, O[u], other0)

    choose = (
        lax.broadcasted_iota(jnp.int32, (LANES, HID), 0)
        == lax.broadcasted_iota(jnp.int32, (LANES, HID), 1) // LANES + g * 3
    ).astype(BF16)
    pick_cols = pl.ds(UNITS[PICK_UNIT][2], LANES)

    def silu(v):
        return 0.5 * v * (1.0 + jnp.tanh(0.5 * v))

    def activate(i, carry):
        gate = acc[i, :, :, :, pl.ds(0, HID)].reshape(256, HID)
        up = acc[i, :, :, :, pl.ds(HID, HID)].reshape(256, HID)
        picks = dot(G[PICK_UNIT][i, :, :, :, pick_cols].reshape(256, LANES), choose)
        hcat[i, :, :, :, pl.ds(0, HID)] = (silu(gate) * up * picks).astype(BF16).reshape(SIDE, SIDE, ROWS, HID)
        return carry

    lax.fori_loop(0, SIDE, activate, 0)
    sg = acc_s[:, pl.ds(0, LANES)]
    su = acc_s[:, pl.ds(LANES, LANES)]
    hcat[x, pl.ds(2 * c, 2), :, :, pl.ds(HID, LANES)] = (
        (silu(sg) * su).astype(BF16).reshape(2, SIDE, ROWS, LANES)
    )

    def rows_of(u, q):
        return hcat[part(UNITS[u][0], 2, q, None, DOWN)].reshape(256, DOWN)

    def give(u, q):
        order, _, cols = UNITS[u]
        block = part(order, 2, q, None, cols)
        return remote(O[u].at[block], S[u].at[block], ss_s.at[u], ss_r.at[u, REL.index(q)], sibling)

    def down_other(u, q):
        order, first, cols = UNITS[u]
        ns = pl.ds(pl.multiple_of(other0 + first, LANES), cols)
        theirs = dot(rows_of(u, q), dcat[:, ns]).astype(BF16)
        O[u][part(order, 2, q, None, cols)] = theirs.reshape(SIDE, SIDE, ROWS, cols)
        give(u, q).start()

    def down_mine(u, q):
        order, first, cols = UNITS[u]
        block = part(order, 2, q, None, cols)
        ns = pl.ds(pl.multiple_of(mine0 + first, LANES), cols)
        mine = dot(rows_of(u, q), dcat[:, ns]).reshape(SIDE, SIDE, ROWS, cols)
        give(u, q).wait_recv()
        G[u][block] = (mine + S[u][block].astype(F32)).astype(BF16)

    def rs_part(k, q, piece, h, order, cols):
        ix = part(order, k, q, piece if k else None, cols)
        return (*ix[:4], halved(cols, h))

    def rs_land(slot, k, piece, h, order, cols):
        ix = landing(slot, order, k, piece if k else None, at, cols)
        return (*ix[:-1], halved(cols, h))

    def rs_sem(k, piece, kind):
        return (16 if k == 0 else (2 - k) * 8 + REL.index(piece) * 2) + min(kind, 1)

    def rs(u, k, piece, kind, step):
        order, _, cols = UNITS[u]
        h = 0 if (step == 1) == (kind != 1) else 1
        slot = 0 if kind == 0 else (1 if step == 1 else 2)
        src = G[u].at[rs_part(k, 2 if kind == 0 else step, piece, h, order, cols)]
        dst = R[u][k].at[rs_land(slot, k, piece, h, order, cols)]
        return remote(src, dst, rs_s.at[u, k], rs_r.at[u, rs_sem(k, piece, kind)], along(order[k], step))

    def rs_far(u, k, piece):
        rs(u, k, piece, 0, 1).start()
        rs(u, k, piece, 0, -1).start()

    def rs_near(u, k, piece, step):
        rs(u, k, piece, 1, step).start()

    def rs_got(u, k, piece, kind):
        ref = blocks_of(G[u], max(k, 1), 2 if kind else 1, UNITS[u][2])
        remote(ref, ref, rs_s.at[u, k], rs_r.at[u, rs_sem(k, piece, kind)], sibling).wait_recv()

    def rs_pass(u, k, piece):
        order, _, cols = UNITS[u]
        rs_got(u, k, piece, 0)
        for h, step in ((0, 1), (1, -1)):
            block = rs_part(k, step, piece, h, order, cols)
            came = R[u][k][rs_land(0, k, piece, h, order, cols)]
            G[u][block] = (G[u][block].astype(F32) + came.astype(F32)).astype(BF16)
            rs(u, k, piece, 2, step).start()

    def rs_sum(u, k, piece):
        order, _, cols = UNITS[u]
        rs_got(u, k, piece, 1)
        block = rs_part(k, 0, piece, None, order, cols)
        l = R[u][k][rs_land(1, k, piece, None, order, cols)]
        r = R[u][k][rs_land(2, k, piece, None, order, cols)]
        total = G[u][block].astype(F32) + (l.astype(F32) + r.astype(F32))
        if k > 0:
            G[u][block] = total.astype(BF16)
            for p in (2, 1, -1, 0) if k == 2 else (0,):
                if piece == 2:
                    rs_far(u, k - 1, p)
                elif piece != 0:
                    rs_near(u, k - 1, p, piece)
        return total

    for u in ALL:
        ag_left(u, 2)
        ref = G[u].at[:, :, :, :, pl.ds(0, UNITS[u][2])]
        remote(ref, ref, as_s.at[u], as_r.at[u, 0], sibling).wait_send()
    for u in ALL:
        down_other(u, 2)
    for u in ALL:
        down_other(u, 1)
    for u in ALL:
        down_mine(u, 2)
        rs_far(u, 2, 2)
        rs_far(u, 2, 1)
    for u in ALL:
        down_other(u, -1)
    for u in ALL:
        down_mine(u, 1)
        rs_near(u, 2, 2, 1)
    for u in ALL:
        down_mine(u, -1)
        rs_near(u, 2, 2, -1)
        rs_far(u, 2, -1)
    for u in ALL:
        rs_near(u, 2, 1, 1)
        rs_near(u, 2, 1, -1)
        rs_far(u, 2, 0)
    for u in ALL:
        rs_pass(u, 2, 2)
    for u in ALL:
        rs_near(u, 2, -1, 1)
        rs_near(u, 2, -1, -1)
    for u in ALL:
        down_other(u, 0)
    for u in ALL:
        rs_pass(u, 2, 1)
    for u in ALL:
        rs_near(u, 2, 0, 1)
        rs_near(u, 2, 0, -1)
    for u in ALL:
        down_mine(u, 0)
    for u in ALL:
        rs_sum(u, 2, 2)
    for u in ALL:
        rs_pass(u, 2, -1)
    for u in ALL:
        rs_sum(u, 2, 1)
    for u in ALL:
        rs_pass(u, 2, 0)
    for u in ALL:
        rs_sum(u, 2, -1)
    for p in (2, 1, -1, 0):
        for u in ALL:
            rs_pass(u, 1, p)
    for u in ALL:
        rs_sum(u, 2, 0)
    for p in (2, 1, -1):
        for u in ALL:
            rs_sum(u, 1, p)
    for u in ALL:
        rs_pass(u, 0, 0)
    for u in ALL:
        rs_sum(u, 1, 0)
    for u in ALL:
        _, first, cols = UNITS[u]
        fs[:, :, pl.ds(first, cols)] = rs_sum(u, 0, 0).reshape(2, 8, cols)

    final = remote(fs.at[o], fr, x_sem.at[2], x_sem.at[3], sibling)
    final.start()
    out[:, pl.ds(pl.multiple_of(mine0, LANES), HALF)] = fs[c].astype(BF16)
    final.wait_recv()
    out[:, pl.ds(pl.multiple_of(other0, LANES), HALF)] = fr[...].astype(BF16)
    final.wait_send()
    for u in ALL:
        for k in range(3):
            ref = blocks_of(G[u], k + 1, 3, UNITS[u][2])
            remote(ref, ref, rs_s.at[u, k], rs_r.at[u, 0], sibling).wait_send()
        remote(O[u], O[u], ss_s.at[u], ss_r.at[u, 0], sibling).wait_send()


def on_device(
    tokens,
    picked_group_index,
    picked_expert_index,
    routing_pick_weight,
    common_gate_weight,
    common_up_weight,
    common_down_weight,
    routed_gate_weight,
    routed_up_weight,
    routed_down_weight,
    gate_block_scales,
    up_block_scales,
    down_block_scales,
    adapter_input_maps,
    adapter_output_maps,
    adapter_down_input,
    adapter_down_output,
):
    vmem = pl.BlockSpec(memory_space=pltpu.VMEM)
    hbm = pl.BlockSpec(memory_space=pl.ANY)
    scratch = []
    for u in range(NU):
        scratch.append(pltpu.VMEM((SIDE, SIDE, SIDE, ROWS, gathered_width(u)), BF16))
    for _ in range(2):
        for _, _, cols in UNITS:
            scratch.append(pltpu.VMEM((SIDE, SIDE, SIDE, ROWS, cols), BF16))
    for _, _, cols in UNITS:
        for k in range(3):
            scratch.append(pltpu.VMEM((3, *([SIDE] * k), ROWS, cols), BF16))
    scratch += [
        pltpu.VMEM((WIDTH, GU), BF16),
        pltpu.VMEM((WIDTH, 2 * LANES), BF16),
        pltpu.VMEM((DOWN, WIDTH), BF16),
        pltpu.VMEM((3, 32, WIDTH), BF16),
        pltpu.VMEM((3, 16, WIDTH), BF16),
        pltpu.VMEM((SIDE, SIDE, SIDE, ROWS, GU), F32),
        pltpu.VMEM((128, 2 * LANES), F32),
        pltpu.VMEM((SIDE, SIDE, SIDE, ROWS, DOWN), BF16),
        pltpu.VMEM((96, GU), BF16),
        pltpu.VMEM((48, HID), BF16),
        pltpu.VMEM((8, HALF + LANES), F32),
        pltpu.VMEM((2, 8, HALF + LANES), F32),
        pltpu.VMEM((2, 8, HALF), F32),
        pltpu.VMEM((8, HALF), F32),
        pltpu.SMEM((3, 1, WIDTH // QB), F32),
        pltpu.SMEM((3, 1, WIDTH // QB), F32),
        pltpu.SMEM((3, 1, WIDTH // QB), F32),
        pltpu.VMEM((8, WIDTH), BF16),
        pltpu.VMEM((8, 8), jnp.int32),
        pltpu.VMEM((8, 8), BF16),
        pltpu.VMEM((3, 2, 16, LANES), BF16),
        pltpu.VMEM((3, 16, LANES), BF16),
        pltpu.SemaphoreType.DMA((8,)),
        pltpu.SemaphoreType.DMA((3,)),
        pltpu.SemaphoreType.DMA((4,)),
        pltpu.SemaphoreType.DMA((4,)),
        pltpu.SemaphoreType.DMA((NU, 3)),
        pltpu.SemaphoreType.DMA((NU, AG_WAITS)),
        pltpu.SemaphoreType.DMA((NU,)),
        pltpu.SemaphoreType.DMA((NU, 5)),
        pltpu.SemaphoreType.DMA((NU, 3)),
        pltpu.SemaphoreType.DMA((NU, 18)),
        pltpu.SemaphoreType.DMA((NU,)),
        pltpu.SemaphoreType.DMA((NU, 4)),
    ]
    return pl.pallas_call(
        kernel,
        out_shape=jax.ShapeDtypeStruct((8, WIDTH), BF16),
        in_specs=[hbm] * 16,
        out_specs=vmem,
        scratch_shapes=scratch,
        compiler_params=pltpu.CompilerParams(
            collective_id=0, has_side_effects=True, vmem_limit_bytes=62 * 2**20
        ),
        cost_estimate=pl.CostEstimate(flops=22 * 10**9, bytes_accessed=25 * 10**6, transcendentals=10**6),
    )(
        gate_block_scales.transpose(0, 2, 1),
        up_block_scales.transpose(0, 2, 1),
        down_block_scales,
        tokens,
        picked_expert_index,
        routing_pick_weight,
        adapter_output_maps,
        adapter_down_input.transpose(0, 2, 1),
        routed_gate_weight,
        routed_up_weight,
        routed_down_weight,
        common_gate_weight,
        common_up_weight,
        common_down_weight,
        adapter_input_maps.transpose(0, 2, 1),
        adapter_down_output,
    )


def solution(mesh):
    in_specs = (
        P(("group", "local"), None),
        P(("group", "local"), None),
        P(("group", "local"), None),
        P(("group", "local"), None),
        P(None, "local"),
        P(None, "local"),
        P("local", None),
        P("group", None, "local"),
        P("group", None, "local"),
        P("group", "local", None),
        P("group", None, "local"),
        P("group", None, "local"),
        P("group", "local", None),
        P("group", None, None),
        P("group", None, None, "local"),
        P("group", "local", None),
        P("group", None, None),
    )
    return jax.shard_map(
        on_device, mesh=mesh, in_specs=in_specs, out_specs=P(("group", "local"), None), check_vma=False
    )
```

```python
import functools

import jax
import jax.numpy as jnp
from jax import lax
from jax.experimental import pallas as pl
from jax.experimental.pallas import tpu as pltpu
from jax.sharding import PartitionSpec as P

MESH = pl.DeviceIdType.MESH
F32 = jnp.float32
BF16 = jnp.bfloat16

WIDTH = 7168
HALF = WIDTH // 2
SIDE = 4
ROWS = 16
QB = 128
LANES = 128
HID = 384
GU = 2 * HID
DOWN = HID + LANES

UNITS = (
    ((0, 1, 2), 0, 1280),
    ((1, 2, 0), 1280, 1280),
    ((2, 0, 1), 2560, 1024),
)
NU = len(UNITS)
PICK_UNIT = 2
REL = (0, 1, -1, 2)

AG_GROUPS = (
    ((0, 0, 0),),
    ((0, 0, 1),),
    ((0, 0, 2), (0, 1, 2)),
    ((1, 0, 0), (1, -1, 1)),
    ((1, 1, 0), (1, 2, 1)),
    ((1, -1, 0), (1, 2, 0)),
    ((1, 0, 1), (1, 1, 1)),
    ((1, 0, 2), (1, 1, 2), (1, -1, 2), (1, 2, 2)),
    ((2, 0, 0), (2, 0, 1)),
    ((2, -1, 0), (2, -1, 1)),
    ((2, 1, 0), (2, 1, 1)),
    ((2, 2, 0), (2, 2, 1)),
    ((2, 0, 2), (2, -1, 2)),
    ((2, 1, 2), (2, 2, 2)),
)
AG_WAITS = len(AG_GROUPS)
AG_GROUP_OF = {copy: i for i, group in enumerate(AG_GROUPS) for copy in group}
HERE = ((None, 0),)
NEAR_A = ((0, -1), (0, 1), (-1, -1), (-1, 1))
NEAR_B = ((1, -1), (1, 1), (2, -1), (2, 1))
FAR = ((0, 2), (-1, 2), (1, 2), (2, 2))
HAND_GROUPS = (HERE, NEAR_A, NEAR_B, FAR)
GIVE_GROUPS = (
    ((2, 2),),
    ((1, 2),),
    ((2, 1), (2, -1)),
    ((-1, 2), (1, 1), (1, -1)),
    ((0, 2), (-1, 1), (-1, -1)),
    ((0, 1), (0, -1)),
    ((2, 0), (1, 0), (-1, 0), (0, 0)),
)


def gathered_width(u):
    return UNITS[u][2] + (LANES if u == PICK_UNIT else 0)


def halved(cols, h):
    if h is None:
        return pl.ds(0, cols)
    cut = cols // 256 * LANES
    return pl.ds(0, cut) if h == 0 else pl.ds(cut, cols - cut)


def landing(slot, order, k, piece, at, cols):
    if k == 0:
        return (slot, pl.ds(0, ROWS), halved(cols, piece))
    whole = sorted(order[:k])
    ix = [pl.ds(0, SIDE)] * k
    if piece is not None:
        ix[whole.index(order[k - 1])] = at(order[k - 1], piece)
    return (slot, *ix, pl.ds(0, ROWS), pl.ds(0, cols))


def dot(a, b):
    return jnp.dot(a, b, preferred_element_type=F32)


def dot_t(a, b):
    return lax.dot_general(a, b, (((0,), (0,)), ((), ())), preferred_element_type=F32)


def kernel(*refs):
    it = iter(refs)

    def take(n):
        return [next(it) for _ in range(n)]

    small_in = take(8)
    (gate_w, up_w, down_w, sgate_w, sup_w, sdown_w, in_t, b_maps) = take(8)
    (out,) = take(1)
    G = take(NU)
    O = take(NU)
    S = take(NU)
    R = [take(3) for _ in range(NU)]
    (gu, sgu, dcat, in_v, b_v, acc, acc_s, hcat, out_bd, a_bd, xs, xf, fs, fr) = take(14)
    small = take(8)
    (gate_s, up_s, down_s, tokens, picked, weight, out_maps, a_t) = small
    (i_sem, w_sem, m_sem, x_sem, ag_s, ag_r, as_s, as_r, rs_s, rs_r, ss_s, ss_r) = take(12)

    g = lax.axis_index("group")
    loc = lax.axis_index("local")
    x, c = g // 2, g % 2
    z, y = loc // SIDE, loc % SIDE
    own = (x, y, z)
    o = 1 - c

    def along(axis, step):
        p = (own[axis] + step + SIDE) % SIDE
        if axis == 0:
            return (p * 2 + c, loc)
        if axis == 1:
            return (g, z * SIDE + p)
        return (g, p * SIDE + y)

    sibling = (x * 2 + o, loc)

    def at(axis, step):
        return (own[axis] + step + SIDE) % SIDE

    def part(order, k, q, piece, cols):
        ix = list(own)
        for a in order[:k]:
            ix[a] = pl.ds(0, SIDE)
        ix[order[k]] = at(order[k], q)
        if k == 0:
            return (*ix, pl.ds(0, ROWS), halved(cols, piece))
        if piece is not None:
            ix[order[k - 1]] = at(order[k - 1], piece)
        return (*ix, pl.ds(0, ROWS), pl.ds(0, cols))

    def remote(src, dst, ss, rs, dev):
        return pltpu.make_async_remote_copy(
            src_ref=src, dst_ref=dst, send_sem=ss, recv_sem=rs, device_id=dev, device_id_type=MESH
        )

    barrier = pltpu.get_barrier_semaphore()
    partners = [along(a, s) for a in range(3) for s in (1, -1)] + [sibling]
    for p in partners:
        pl.semaphore_signal(barrier, inc=1, device_id=p, device_id_type=MESH)

    inward = [pltpu.make_async_copy(a, b, i_sem.at[i]) for i, (a, b) in enumerate(zip(small_in, small))]
    for i in (3, 4, 5, 6, 7, 0, 1, 2):
        inward[i].start()
    mine0 = c * HALF
    other0 = o * HALF
    w_rows = ((mine0, HALF // 2), (mine0 + HALF // 2, HALF // 2), (other0, HALF))

    def w_copy(i, j):
        rows = pl.ds(*w_rows[i])
        src = (gate_w if j < 3 else up_w).at[j % 3, rows]
        return pltpu.make_async_copy(src, gu.at[rows, pl.ds(j * LANES, LANES)], w_sem.at[i])

    def m_copy(i):
        if i == 0:
            return pltpu.make_async_copy(in_t, in_v, m_sem.at[0])
        if i < 3:
            src = sgate_w if i == 1 else sup_w
            return pltpu.make_async_copy(src, sgu.at[:, pl.ds((i - 1) * LANES, LANES)], m_sem.at[1])
        if i == 3:
            return pltpu.make_async_copy(b_maps, b_v, m_sem.at[2])
        if i == 4:
            return pltpu.make_async_copy(sdown_w, dcat.at[pl.ds(HID, LANES)], m_sem.at[3])
        return pltpu.make_async_copy(down_w.at[i - 5], dcat.at[pl.ds((i - 5) * LANES, LANES)], m_sem.at[3])

    def wait_all(ref, sem):
        pltpu.make_async_copy(ref, ref, sem).wait()

    m_copy(0).start()
    for j in range(6):
        w_copy(0, j).start()

    out_bd[...] = jnp.zeros_like(out_bd)
    a_bd[...] = jnp.zeros_like(a_bd)
    hcat[:, :, :, :, pl.ds(HID, LANES)] = jnp.zeros((SIDE, SIDE, SIDE, ROWS, LANES), BF16)
    for i in (3, 4, 5):
        inward[i].wait()
    lane = lax.broadcasted_iota(jnp.int32, (8, LANES), 1)
    pick = jnp.zeros((8, LANES), F32)
    for k in range(8):
        pick = pick + jnp.where(lane == picked[:, k : k + 1], weight[:, k : k + 1].astype(F32), 0.0)
    xs[:, pl.ds(0, HALF)] = tokens[:, pl.ds(pl.multiple_of(other0, LANES), HALF)].astype(F32)
    xs[:, pl.ds(HALF, LANES)] = pick
    xf[c, :, pl.ds(0, HALF)] = tokens[:, pl.ds(pl.multiple_of(mine0, LANES), HALF)].astype(F32)
    xf[c, :, pl.ds(HALF, LANES)] = pick
    pl.semaphore_wait(barrier, len(partners))
    swap = remote(xs, xf.at[c], x_sem.at[0], x_sem.at[1], sibling)
    swap.start()

    for i in (1, 2):
        for j in range(6):
            w_copy(i, j).start()
    for i in range(1, 8):
        m_copy(i).start()
    for i in (6, 7, 0, 1, 2):
        inward[i].wait()
    for e in range(3):
        for h in range(2):
            out_bd[pl.ds(e * 32 + h * 16, 16), pl.ds((h * 3 + e) * LANES, LANES)] = out_maps[e, h]
        a_bd[pl.ds(e * 16, 16), pl.ds(e * LANES, LANES)] = a_t[e]
    swap.wait_send()
    remote(xs, xf.at[o], x_sem.at[0], x_sem.at[1], sibling).wait_recv()
    block = xf[...].reshape(ROWS, HALF + LANES).astype(BF16)
    for u, (order, first, cols) in enumerate(UNITS):
        G[u][x, y, z, :, pl.ds(0, cols)] = block[:, first : first + cols]
        if u == PICK_UNIT:
            G[u][x, y, z, :, pl.ds(cols, LANES)] = block[:, HALF:]

    def ag(u, k, piece, kind, arriving=False):
        order = UNITS[u][0]
        if kind == 2:
            step = 1 if piece in ((0,) if k == 0 else (0, 1)) else -1
            q = -2 * step if arriving else -step
        else:
            step = 1 if kind == 0 else -1
            q = -step if arriving else 0
        which = None if k == 0 and kind < 2 else piece
        block = G[u].at[part(order, k, q, which, gathered_width(u))]
        sem = AG_GROUP_OF[(k, piece, kind)]
        return remote(block, block, ag_s.at[u, k], ag_r.at[u, sem], along(order[k], step))

    def ag_send(u, k, piece):
        ag(u, k, piece, 0).start()
        ag(u, k, piece, 1).start()

    def blocks_of(ref, k, n, cols):
        ix = [0, 0, 0, pl.ds(0, ROWS), pl.ds(0, cols)]
        if k > 0:
            ix[3 - k] = pl.ds(0, n)
            for j in range(4 - k, 3):
                ix[j] = pl.ds(0, SIDE)
        return ref.at[tuple(ix)]

    def ag_got(u, i):
        k, _, kind = AG_GROUPS[i][0]
        n = len(AG_GROUPS[i])
        if k == 0:
            n = 1
        ref = blocks_of(G[u], max(k, 1), n, gathered_width(u))
        remote(ref, ref, ag_s.at[u, k], ag_r.at[u, i], sibling).wait_recv()

    def ag_pass(u, k, piece):
        ag(u, k, piece, 2).start()

    def ag_left(u, k):
        ref = blocks_of(G[u], k + 1, 3, gathered_width(u))
        remote(ref, ref, ag_s.at[u, k], ag_r.at[u, 0], sibling).wait_send()

    def ag_block(u, j):
        order = UNITS[u][0]
        ix = list(part(order, 2, 0, 0, gathered_width(u)))
        ix[order[0]] = at(order[0], j)
        block = G[u].at[tuple(ix)]
        for kind, step in ((0, 1), (1, -1)):
            sem = AG_GROUP_OF[(2, 0, kind)]
            remote(block, block, ag_s.at[u, 2], ag_r.at[u, sem], along(order[2], step)).start()

    def line_a(u):
        ag_got(u, 0)
        ag_pass(u, 0, 0)
        ag_send(u, 1, -1)
        ag_got(u, 1)
        ag_pass(u, 0, 1)
        ag_send(u, 1, 1)

    def line_b(u):
        ag_got(u, 2)
        ag_send(u, 1, 2)
        ag_block(u, 2)

    def plane_a(u):
        ag_got(u, 3)
        ag_pass(u, 1, 0)
        ag_pass(u, 1, -1)
        ag_got(u, 4)
        ag_pass(u, 1, 1)
        ag_pass(u, 1, 2)

    def plane_b(u):
        ag_got(u, 5)
        ag_send(u, 2, -1)
        ag_got(u, 6)
        ag_send(u, 2, 1)

    def plane_c(u):
        ag_got(u, 7)
        ag_send(u, 2, 2)
        hand(u, None, 0).start()

    def cube_a(u, piece):
        ag_got(u, {0: 8, -1: 9, 1: 10, 2: 11}[piece])
        ag_pass(u, 2, piece)
        hand(u, piece, -1).start()
        hand(u, piece, 1).start()

    def cube_b(u, i):
        ag_got(u, 12 + i)
        for r, q in FAR[2 * i : 2 * i + 2]:
            hand(u, r, q).start()

    def hand(u, piece, q):
        order, _, cols = UNITS[u]
        block = part(order, 2, q, piece, cols)
        (i,) = (i for i, rows in enumerate(HAND_GROUPS) if (piece, q) in rows)
        return remote(G[u].at[block], O[u].at[block], as_s.at[u], as_r.at[u, i], sibling)

    def gate_up(u, src, first0, rows):
        order, first, cols = UNITS[u]
        if rows is FAR:
            rows = ((None, 2),)
        ws = pl.ds(pl.multiple_of(first0 + first, LANES), cols)
        if len(rows) == 1:
            lhs = src[part(order, 2, rows[0][1], None, cols)].reshape(256, cols)
            at_a = part(order, 2, rows[0][1], None, GU)
            acc[at_a] = acc[at_a] + dot(lhs, gu[ws, :]).reshape(SIDE, SIDE, ROWS, GU)
            return
        lhs = jnp.concatenate([src[part(order, 2, q, r, cols)].reshape(64, cols) for r, q in rows], axis=0)
        got = dot(lhs, gu[ws, :])
        for i, (r, q) in enumerate(rows):
            at_a = part(order, 2, q, r, GU)
            acc[at_a] = acc[at_a] + got[i * 64 : (i + 1) * 64].reshape(SIDE, ROWS, GU)

    def from_sibling(u, rows):
        n = SIDE if rows is HERE else len(rows)
        ref = blocks_of(O[u], 2, n, UNITS[u][2])
        remote(ref, ref, as_s.at[u], as_r.at[u, HAND_GROUPS.index(rows)], sibling).wait_recv()
        gate_up(u, O[u], other0, rows)

    def shared(u, src, first0):
        _, first, cols = UNITS[u]
        ws = pl.ds(pl.multiple_of(first0 + first, LANES), cols)
        acc_s[...] += dot(src[x, pl.ds(2 * c, 2), :, :, pl.ds(0, cols)].reshape(128, cols), sgu[ws, :])

    def merge_up(first, n):
        def body(i, carry):
            kb = first + i * 4
            ab = dot_t(in_v[:, :, pl.ds(pl.multiple_of(kb * QB, QB), 4 * QB)].reshape(96, 4 * QB), out_bd[...])
            for t in range(4):
                ks = pl.ds(pl.multiple_of(kb * QB, QB) + t * QB, QB)
                for j in range(6):
                    cs = pl.ds(j * LANES, LANES)
                    s = (gate_s if j < 3 else up_s)[j % 3, 0, kb + t]
                    add = ab[t * QB : (t + 1) * QB, j * LANES : (j + 1) * LANES]
                    gu[ks, cs] = (gu[ks, cs].astype(F32) * s + add).astype(BF16)
            return carry

        lax.fori_loop(0, n, body, 0)

    def merge_down(first, n):
        def body(i, carry):
            n0 = pl.multiple_of((first + i) * 1024, 1024)
            ab = dot_t(a_bd[...], b_v[:, :, pl.ds(n0, 1024)].reshape(48, 1024))
            for e in range(3):
                for t in range(8):
                    at_d = (pl.ds(e * LANES, LANES), pl.ds(n0 + t * QB, QB))
                    s = down_s[e, 0, (first + i) * 8 + t]
                    add = ab[e * LANES : (e + 1) * LANES, t * QB : (t + 1) * QB]
                    dcat[at_d] = (dcat[at_d].astype(F32) * s + add).astype(BF16)
            return carry

        lax.fori_loop(0, n, body, 0)

    def wait_w(i):
        wait_all(gu.at[pl.ds(*w_rows[i])], w_sem.at[i])

    ALL = range(NU)
    for u in ALL:
        ag_send(u, 0, 0)
    for u in ALL:
        ag_send(u, 1, 0)
    for u in ALL:
        ag_block(u, 0)
    acc[...] = jnp.zeros_like(acc)
    acc_s[...] = jnp.zeros_like(acc_s)
    m_copy(0).wait()
    wait_w(0)
    merge_up(c * 28, 2)
    for u in ALL:
        line_a(u)
    for u in ALL:
        ag_block(u, -1)
        ag_block(u, 1)
    merge_up(c * 28 + 8, 1)
    wait_w(1)
    merge_up(c * 28 + 12, 2)
    for u in ALL:
        line_b(u)
    merge_up(c * 28 + 20, 2)
    wait_w(2)
    merge_up(o * 28, 1)
    for u in ALL:
        plane_a(u)
    merge_up(o * 28 + 4, 3)
    for u in ALL:
        plane_b(u)
    merge_up(o * 28 + 16, 3)
    m_copy(3).wait()
    wait_all(dcat, m_sem.at[3])
    merge_down(0, 2)
    for u in ALL:
        plane_c(u)
    for u in ALL:
        gate_up(u, G[u], mine0, HERE)
    for u in ALL:
        cube_a(u, 0)
    for u in ALL:
        from_sibling(u, HERE)
    for u in ALL:
        cube_a(u, -1)
    merge_down(2, 2)
    for u in ALL:
        gate_up(u, G[u], mine0, NEAR_A)
    for u in ALL:
        cube_a(u, 1)
    for u in ALL:
        from_sibling(u, NEAR_A)
    for u in ALL:
        cube_a(u, 2)
    for u in ALL:
        gate_up(u, G[u], mine0, NEAR_B)
    merge_down(4, 3)
    for u in ALL:
        from_sibling(u, NEAR_B)
    wait_all(sgu, m_sem.at[1])
    for u in ALL:
        cube_b(u, 0)
    for u in ALL:
        for k in (0, 1):
            ag_left(u, k)
    for u in ALL:
        cube_b(u, 1)
    for u in ALL:
        gate_up(u, G[u], mine0, FAR)
    for u in ALL:
        shared(u, G[u], mine0)
    for u in ALL:
        from_sibling(u, FAR)
        shared(u, O[u], other0)

    choose = (
        lax.broadcasted_iota(jnp.int32, (LANES, HID), 0)
        == lax.broadcasted_iota(jnp.int32, (LANES, HID), 1) // LANES + g * 3
    ).astype(BF16)
    pick_cols = pl.ds(UNITS[PICK_UNIT][2], LANES)

    def silu(v):
        return 0.5 * v * (1.0 + jnp.tanh(0.5 * v))

    def activate(i, carry):
        gate = acc[i, :, :, :, pl.ds(0, HID)].reshape(256, HID)
        up = acc[i, :, :, :, pl.ds(HID, HID)].reshape(256, HID)
        picks = dot(G[PICK_UNIT][i, :, :, :, pick_cols].reshape(256, LANES), choose)
        hcat[i, :, :, :, pl.ds(0, HID)] = (silu(gate) * up * picks).astype(BF16).reshape(SIDE, SIDE, ROWS, HID)
        return carry

    lax.fori_loop(0, SIDE, activate, 0)
    sg = acc_s[:, pl.ds(0, LANES)]
    su = acc_s[:, pl.ds(LANES, LANES)]
    hcat[x, pl.ds(2 * c, 2), :, :, pl.ds(HID, LANES)] = (
        (silu(sg) * su).astype(BF16).reshape(2, SIDE, ROWS, LANES)
    )

    def rows_of(u, q):
        return hcat[part(UNITS[u][0], 2, q, None, DOWN)].reshape(256, DOWN)

    def give(u, r, q):
        order, _, cols = UNITS[u]
        block = part(order, 2, q, r, cols)
        (i,) = (i for i, rows in enumerate(GIVE_GROUPS) if (r, q) in rows)
        return remote(O[u].at[block], S[u].at[block], ss_s.at[u], ss_r.at[u, i], sibling)

    def down_other(u, q):
        order, first, cols = UNITS[u]
        ns = pl.ds(pl.multiple_of(other0 + first, LANES), cols)
        theirs = dot(rows_of(u, q), dcat[:, ns]).astype(BF16)
        O[u][part(order, 2, q, None, cols)] = theirs.reshape(SIDE, SIDE, ROWS, cols)

    def down_mine(u, q):
        order, first, cols = UNITS[u]
        ns = pl.ds(pl.multiple_of(mine0 + first, LANES), cols)
        mine = dot(rows_of(u, q), dcat[:, ns]).astype(BF16)
        G[u][part(order, 2, q, None, cols)] = mine.reshape(SIDE, SIDE, ROWS, cols)

    def take_in(u, i):
        order, _, cols = UNITS[u]
        ref = blocks_of(S[u], 2, len(GIVE_GROUPS[i]), cols)
        remote(ref, ref, ss_s.at[u], ss_r.at[u, i], sibling).wait_recv()
        for r, q in GIVE_GROUPS[i]:
            block = part(order, 2, q, r, cols)
            G[u][block] = (G[u][block].astype(F32) + S[u][block].astype(F32)).astype(BF16)

    def rs_part(k, q, piece, h, order, cols):
        ix = part(order, k, q, piece if k else None, cols)
        return (*ix[:4], halved(cols, h))

    def rs_land(slot, k, piece, h, order, cols):
        ix = landing(slot, order, k, piece if k else None, at, cols)
        return (*ix[:-1], halved(cols, h))

    def rs_sem(k, piece, kind):
        return (16 if k == 0 else (2 - k) * 8 + REL.index(piece) * 2) + min(kind, 1)

    def rs(u, k, piece, kind, step):
        order, _, cols = UNITS[u]
        h = 0 if (step == 1) == (kind != 1) else 1
        slot = 0 if kind == 0 else (1 if step == 1 else 2)
        src = G[u].at[rs_part(k, 2 if kind == 0 else step, piece, h, order, cols)]
        dst = R[u][k].at[rs_land(slot, k, piece, h, order, cols)]
        return remote(src, dst, rs_s.at[u, k], rs_r.at[u, rs_sem(k, piece, kind)], along(order[k], step))

    def rs_far(u, k, piece):
        rs(u, k, piece, 0, 1).start()
        rs(u, k, piece, 0, -1).start()

    def rs_near(u, k, piece, step):
        rs(u, k, piece, 1, step).start()

    def rs_got(u, k, piece, kind):
        ref = blocks_of(G[u], max(k, 1), 2 if kind else 1, UNITS[u][2])
        remote(ref, ref, rs_s.at[u, k], rs_r.at[u, rs_sem(k, piece, kind)], sibling).wait_recv()

    def rs_pass(u, k, piece):
        order, _, cols = UNITS[u]
        rs_got(u, k, piece, 0)
        for h, step in ((0, 1), (1, -1)):
            block = rs_part(k, step, piece, h, order, cols)
            came = R[u][k][rs_land(0, k, piece, h, order, cols)]
            G[u][block] = (G[u][block].astype(F32) + came.astype(F32)).astype(BF16)
            rs(u, k, piece, 2, step).start()

    def rs_sum(u, k, piece):
        order, _, cols = UNITS[u]
        rs_got(u, k, piece, 1)
        block = rs_part(k, 0, piece, None, order, cols)
        l = R[u][k][rs_land(1, k, piece, None, order, cols)]
        r = R[u][k][rs_land(2, k, piece, None, order, cols)]
        total = G[u][block].astype(F32) + (l.astype(F32) + r.astype(F32))
        if k > 0:
            G[u][block] = total.astype(BF16)
            for p in (2, 1, -1, 0) if k == 2 else (0,):
                if piece == 2:
                    rs_far(u, k - 1, p)
                elif piece != 0:
                    rs_near(u, k - 1, p, piece)
        return total

    for u in ALL:
        down_other(u, 2)
        give(u, 2, 2).start()
        give(u, 1, 2).start()
    for u in ALL:
        ag_left(u, 2)
        ref = G[u].at[:, :, :, :, pl.ds(0, UNITS[u][2])]
        remote(ref, ref, as_s.at[u], as_r.at[u, 0], sibling).wait_send()
    for u in ALL:
        down_mine(u, 2)
        take_in(u, 0)
        rs_far(u, 2, 2)
    for q in (1, -1):
        for u in ALL:
            down_other(u, q)
            give(u, 2, q).start()
    for u in ALL:
        take_in(u, 1)
        rs_far(u, 2, 1)
    for u in ALL:
        for r, q in GIVE_GROUPS[3]:
            give(u, r, q).start()
    for u in ALL:
        down_mine(u, 1)
        down_mine(u, -1)
        take_in(u, 2)
        rs_near(u, 2, 2, 1)
        rs_near(u, 2, 2, -1)
    for u in ALL:
        for r, q in GIVE_GROUPS[4]:
            give(u, r, q).start()
    for u in ALL:
        rs_pass(u, 2, 2)
        take_in(u, 3)
        rs_far(u, 2, -1)
        rs_near(u, 2, 1, 1)
        rs_near(u, 2, 1, -1)
    for u in ALL:
        for r, q in GIVE_GROUPS[5]:
            give(u, r, q).start()
    for u in ALL:
        down_other(u, 0)
        for r, q in GIVE_GROUPS[6]:
            give(u, r, q).start()
    for u in ALL:
        rs_pass(u, 2, 1)
        take_in(u, 4)
        rs_far(u, 2, 0)
        rs_near(u, 2, -1, 1)
        rs_near(u, 2, -1, -1)
    for u in ALL:
        down_mine(u, 0)
        take_in(u, 6)
    for u in ALL:
        rs_sum(u, 2, 2)
    for u in ALL:
        rs_pass(u, 2, -1)
        take_in(u, 5)
        rs_near(u, 2, 0, 1)
        rs_near(u, 2, 0, -1)
    for u in ALL:
        rs_sum(u, 2, 1)
    for u in ALL:
        rs_pass(u, 2, 0)
    for u in ALL:
        rs_sum(u, 2, -1)
    for p in (2, 1, -1, 0):
        for u in ALL:
            rs_pass(u, 1, p)
    for u in ALL:
        rs_sum(u, 2, 0)
    for p in (2, 1, -1):
        for u in ALL:
            rs_sum(u, 1, p)
    for u in ALL:
        rs_pass(u, 0, 0)
    for u in ALL:
        rs_sum(u, 1, 0)
    for u in ALL:
        _, first, cols = UNITS[u]
        fs[:, :, pl.ds(first, cols)] = rs_sum(u, 0, 0).reshape(2, 8, cols)

    final = remote(fs.at[o], fr, x_sem.at[2], x_sem.at[3], sibling)
    final.start()
    out[:, pl.ds(pl.multiple_of(mine0, LANES), HALF)] = fs[c].astype(BF16)
    final.wait_recv()
    out[:, pl.ds(pl.multiple_of(other0, LANES), HALF)] = fr[...].astype(BF16)
    final.wait_send()
    for u in ALL:
        for k in range(3):
            ref = blocks_of(G[u], k + 1, 3, UNITS[u][2])
            remote(ref, ref, rs_s.at[u, k], rs_r.at[u, 0], sibling).wait_send()
        remote(O[u], O[u], ss_s.at[u], ss_r.at[u, 0], sibling).wait_send()


def on_device(
    tokens,
    picked_group_index,
    picked_expert_index,
    routing_pick_weight,
    common_gate_weight,
    common_up_weight,
    common_down_weight,
    routed_gate_weight,
    routed_up_weight,
    routed_down_weight,
    gate_block_scales,
    up_block_scales,
    down_block_scales,
    adapter_input_maps,
    adapter_output_maps,
    adapter_down_input,
    adapter_down_output,
):
    vmem = pl.BlockSpec(memory_space=pltpu.VMEM)
    hbm = pl.BlockSpec(memory_space=pl.ANY)
    scratch = []
    for u in range(NU):
        scratch.append(pltpu.VMEM((SIDE, SIDE, SIDE, ROWS, gathered_width(u)), BF16))
    for _ in range(2):
        for _, _, cols in UNITS:
            scratch.append(pltpu.VMEM((SIDE, SIDE, SIDE, ROWS, cols), BF16))
    for _, _, cols in UNITS:
        for k in range(3):
            scratch.append(pltpu.VMEM((3, *([SIDE] * k), ROWS, cols), BF16))
    scratch += [
        pltpu.VMEM((WIDTH, GU), BF16),
        pltpu.VMEM((WIDTH, 2 * LANES), BF16),
        pltpu.VMEM((DOWN, WIDTH), BF16),
        pltpu.VMEM((3, 32, WIDTH), BF16),
        pltpu.VMEM((3, 16, WIDTH), BF16),
        pltpu.VMEM((SIDE, SIDE, SIDE, ROWS, GU), F32),
        pltpu.VMEM((128, 2 * LANES), F32),
        pltpu.VMEM((SIDE, SIDE, SIDE, ROWS, DOWN), BF16),
        pltpu.VMEM((96, GU), BF16),
        pltpu.VMEM((48, HID), BF16),
        pltpu.VMEM((8, HALF + LANES), F32),
        pltpu.VMEM((2, 8, HALF + LANES), F32),
        pltpu.VMEM((2, 8, HALF), F32),
        pltpu.VMEM((8, HALF), F32),
        pltpu.SMEM((3, 1, WIDTH // QB), F32),
        pltpu.SMEM((3, 1, WIDTH // QB), F32),
        pltpu.SMEM((3, 1, WIDTH // QB), F32),
        pltpu.VMEM((8, WIDTH), BF16),
        pltpu.VMEM((8, 8), jnp.int32),
        pltpu.VMEM((8, 8), BF16),
        pltpu.VMEM((3, 2, 16, LANES), BF16),
        pltpu.VMEM((3, 16, LANES), BF16),
        pltpu.SemaphoreType.DMA((8,)),
        pltpu.SemaphoreType.DMA((3,)),
        pltpu.SemaphoreType.DMA((4,)),
        pltpu.SemaphoreType.DMA((4,)),
        pltpu.SemaphoreType.DMA((NU, 3)),
        pltpu.SemaphoreType.DMA((NU, AG_WAITS)),
        pltpu.SemaphoreType.DMA((NU,)),
        pltpu.SemaphoreType.DMA((NU, 4)),
        pltpu.SemaphoreType.DMA((NU, 3)),
        pltpu.SemaphoreType.DMA((NU, 18)),
        pltpu.SemaphoreType.DMA((NU,)),
        pltpu.SemaphoreType.DMA((NU, 7)),
    ]
    return pl.pallas_call(
        kernel,
        out_shape=jax.ShapeDtypeStruct((8, WIDTH), BF16),
        in_specs=[hbm] * 16,
        out_specs=vmem,
        scratch_shapes=scratch,
        compiler_params=pltpu.CompilerParams(
            collective_id=0, has_side_effects=True, vmem_limit_bytes=62 * 2**20
        ),
        cost_estimate=pl.CostEstimate(flops=22 * 10**9, bytes_accessed=25 * 10**6, transcendentals=10**6),
    )(
        gate_block_scales.transpose(0, 2, 1),
        up_block_scales.transpose(0, 2, 1),
        down_block_scales,
        tokens,
        picked_expert_index,
        routing_pick_weight,
        adapter_output_maps,
        adapter_down_input.transpose(0, 2, 1),
        routed_gate_weight,
        routed_up_weight,
        routed_down_weight,
        common_gate_weight,
        common_up_weight,
        common_down_weight,
        adapter_input_maps.transpose(0, 2, 1),
        adapter_down_output,
    )


def solution(mesh):
    in_specs = (
        P(("group", "local"), None),
        P(("group", "local"), None),
        P(("group", "local"), None),
        P(("group", "local"), None),
        P(None, "local"),
        P(None, "local"),
        P("local", None),
        P("group", None, "local"),
        P("group", None, "local"),
        P("group", "local", None),
        P("group", None, "local"),
        P("group", None, "local"),
        P("group", "local", None),
        P("group", None, None),
        P("group", None, None, "local"),
        P("group", "local", None),
        P("group", None, None),
    )
    return jax.shard_map(
        on_device, mesh=mesh, in_specs=in_specs, out_specs=P(("group", "local"), None), check_vma=False
    )
```

```python
import functools

import jax
import jax.numpy as jnp
from jax import lax
from jax.experimental import pallas as pl
from jax.experimental.pallas import tpu as pltpu
from jax.sharding import PartitionSpec as P

MESH = pl.DeviceIdType.MESH
F32 = jnp.float32
BF16 = jnp.bfloat16

WIDTH = 7168
HALF = WIDTH // 2
SIDE = 4
ROWS = 16
QB = 128
LANES = 128
HID = 384
GU = 2 * HID
DOWN = HID + LANES

UNITS = (
    ((0, 1, 2), 0, 1280),
    ((1, 2, 0), 1280, 1280),
    ((2, 0, 1), 2560, 1024),
)
NU = len(UNITS)
PICK_UNIT = 2
REL = (0, 1, -1, 2)

AG_GROUPS = (
    ((0, 0, 0),),
    ((0, 0, 1),),
    ((0, 0, 2), (0, 1, 2)),
    ((1, 0, 0), (1, -1, 1)),
    ((1, 1, 0), (1, 2, 1)),
    ((1, -1, 0), (1, 2, 0)),
    ((1, 0, 1), (1, 1, 1)),
    ((1, 0, 2), (1, 1, 2), (1, -1, 2), (1, 2, 2)),
    ((2, 0, 0), (2, 0, 1)),
    ((2, -1, 0), (2, -1, 1)),
    ((2, 1, 0), (2, 1, 1)),
    ((2, 2, 0), (2, 2, 1)),
    ((2, 0, 2), (2, -1, 2)),
    ((2, 1, 2), (2, 2, 2)),
)
AG_WAITS = len(AG_GROUPS)
AG_GROUP_OF = {copy: i for i, group in enumerate(AG_GROUPS) for copy in group}
HERE = ((None, 0),)
NEAR_A = ((0, -1), (0, 1), (-1, -1), (-1, 1))
NEAR_B = ((1, -1), (1, 1), (2, -1), (2, 1))
FAR = ((0, 2), (-1, 2), (1, 2), (2, 2))
HAND_GROUPS = (HERE, NEAR_A, NEAR_B, FAR)
GIVE_GROUPS = (
    ((2, 2),),
    ((1, 2),),
    ((-1, 2),),
    ((2, 1), (2, -1)),
    ((1, 1), (1, -1)),
    ((0, 2), (-1, 1), (-1, -1)),
    ((0, 1), (0, -1)),
    ((2, 0), (1, 0), (-1, 0), (0, 0)),
)


def gathered_width(u):
    return UNITS[u][2] + (LANES if u == PICK_UNIT else 0)


def halved(cols, h):
    if h is None:
        return pl.ds(0, cols)
    cut = cols // 256 * LANES
    return pl.ds(0, cut) if h == 0 else pl.ds(cut, cols - cut)


def landing(slot, order, k, piece, at, cols):
    if k == 0:
        return (slot, pl.ds(0, ROWS), halved(cols, piece))
    whole = sorted(order[:k])
    ix = [pl.ds(0, SIDE)] * k
    if piece is not None:
        ix[whole.index(order[k - 1])] = at(order[k - 1], piece)
    return (slot, *ix, pl.ds(0, ROWS), pl.ds(0, cols))


def dot(a, b):
    return jnp.dot(a, b, preferred_element_type=F32)


def dot_t(a, b):
    return lax.dot_general(a, b, (((0,), (0,)), ((), ())), preferred_element_type=F32)


def kernel(*refs):
    it = iter(refs)

    def take(n):
        return [next(it) for _ in range(n)]

    small_in = take(8)
    (gate_w, up_w, down_w, sgate_w, sup_w, sdown_w, in_t, b_maps) = take(8)
    (out,) = take(1)
    G = take(NU)
    O = take(NU)
    S = take(NU)
    R = [take(3) for _ in range(NU)]
    (gu, sgu, dcat, in_v, b_v, acc, acc_s, hcat, out_bd, a_bd, xs, xf, fs, fr) = take(14)
    small = take(8)
    (gate_s, up_s, down_s, tokens, picked, weight, out_maps, a_t) = small
    (i_sem, w_sem, m_sem, x_sem, ag_s, ag_r, as_s, as_r, rs_s, rs_r, ss_s, ss_r) = take(12)

    g = lax.axis_index("group")
    loc = lax.axis_index("local")
    x, c = g // 2, g % 2
    z, y = loc // SIDE, loc % SIDE
    own = (x, y, z)
    o = 1 - c

    def along(axis, step):
        p = (own[axis] + step + SIDE) % SIDE
        if axis == 0:
            return (p * 2 + c, loc)
        if axis == 1:
            return (g, z * SIDE + p)
        return (g, p * SIDE + y)

    sibling = (x * 2 + o, loc)

    def at(axis, step):
        return (own[axis] + step + SIDE) % SIDE

    def part(order, k, q, piece, cols):
        ix = list(own)
        for a in order[:k]:
            ix[a] = pl.ds(0, SIDE)
        ix[order[k]] = at(order[k], q)
        if k == 0:
            return (*ix, pl.ds(0, ROWS), halved(cols, piece))
        if piece is not None:
            ix[order[k - 1]] = at(order[k - 1], piece)
        return (*ix, pl.ds(0, ROWS), pl.ds(0, cols))

    def remote(src, dst, ss, rs, dev):
        return pltpu.make_async_remote_copy(
            src_ref=src, dst_ref=dst, send_sem=ss, recv_sem=rs, device_id=dev, device_id_type=MESH
        )

    barrier = pltpu.get_barrier_semaphore()
    partners = [along(a, s) for a in range(3) for s in (1, -1, 2)] + [sibling]
    for p in partners:
        pl.semaphore_signal(barrier, inc=1, device_id=p, device_id_type=MESH)

    inward = [pltpu.make_async_copy(a, b, i_sem.at[i]) for i, (a, b) in enumerate(zip(small_in, small))]
    for i in (3, 4, 5, 6, 7, 0, 1, 2):
        inward[i].start()
    mine0 = c * HALF
    other0 = o * HALF
    w_rows = ((mine0, HALF // 2), (mine0 + HALF // 2, HALF // 2), (other0, HALF))

    def w_copy(i, j):
        rows = pl.ds(*w_rows[i])
        src = (gate_w if j < 3 else up_w).at[j % 3, rows]
        return pltpu.make_async_copy(src, gu.at[rows, pl.ds(j * LANES, LANES)], w_sem.at[i])

    def m_copy(i):
        if i == 0:
            return pltpu.make_async_copy(in_t, in_v, m_sem.at[0])
        if i < 3:
            src = sgate_w if i == 1 else sup_w
            return pltpu.make_async_copy(src, sgu.at[:, pl.ds((i - 1) * LANES, LANES)], m_sem.at[1])
        if i == 3:
            return pltpu.make_async_copy(b_maps, b_v, m_sem.at[2])
        if i == 4:
            return pltpu.make_async_copy(sdown_w, dcat.at[pl.ds(HID, LANES)], m_sem.at[3])
        return pltpu.make_async_copy(down_w.at[i - 5], dcat.at[pl.ds((i - 5) * LANES, LANES)], m_sem.at[3])

    def wait_all(ref, sem):
        pltpu.make_async_copy(ref, ref, sem).wait()

    m_copy(0).start()
    for j in range(6):
        w_copy(0, j).start()

    out_bd[...] = jnp.zeros_like(out_bd)
    a_bd[...] = jnp.zeros_like(a_bd)
    hcat[:, :, :, :, pl.ds(HID, LANES)] = jnp.zeros((SIDE, SIDE, SIDE, ROWS, LANES), BF16)
    for i in (3, 4, 5):
        inward[i].wait()
    lane = lax.broadcasted_iota(jnp.int32, (8, LANES), 1)
    pick = jnp.zeros((8, LANES), F32)
    for k in range(8):
        pick = pick + jnp.where(lane == picked[:, k : k + 1], weight[:, k : k + 1].astype(F32), 0.0)
    xs[:, pl.ds(0, HALF)] = tokens[:, pl.ds(pl.multiple_of(other0, LANES), HALF)].astype(F32)
    xs[:, pl.ds(HALF, LANES)] = pick
    xf[c, :, pl.ds(0, HALF)] = tokens[:, pl.ds(pl.multiple_of(mine0, LANES), HALF)].astype(F32)
    xf[c, :, pl.ds(HALF, LANES)] = pick
    pl.semaphore_wait(barrier, len(partners))
    swap = remote(xs, xf.at[c], x_sem.at[0], x_sem.at[1], sibling)
    swap.start()

    for i in (1, 2):
        for j in range(6):
            w_copy(i, j).start()
    for i in range(1, 8):
        m_copy(i).start()
    for i in (6, 7, 0, 1, 2):
        inward[i].wait()
    for e in range(3):
        for h in range(2):
            out_bd[pl.ds(e * 32 + h * 16, 16), pl.ds((h * 3 + e) * LANES, LANES)] = out_maps[e, h]
        a_bd[pl.ds(e * 16, 16), pl.ds(e * LANES, LANES)] = a_t[e]
    swap.wait_send()
    remote(xs, xf.at[o], x_sem.at[0], x_sem.at[1], sibling).wait_recv()
    block = xf[...].reshape(ROWS, HALF + LANES).astype(BF16)
    for u, (order, first, cols) in enumerate(UNITS):
        G[u][x, y, z, :, pl.ds(0, cols)] = block[:, first : first + cols]
        if u == PICK_UNIT:
            G[u][x, y, z, :, pl.ds(cols, LANES)] = block[:, HALF:]

    def ag(u, k, piece, kind, arriving=False):
        order = UNITS[u][0]
        if kind == 2:
            step = 1 if piece in ((0,) if k == 0 else (0, 1)) else -1
            q = -2 * step if arriving else -step
        else:
            step = 1 if kind == 0 else -1
            q = -step if arriving else 0
        which = None if k == 0 and kind < 2 else piece
        block = G[u].at[part(order, k, q, which, gathered_width(u))]
        sem = AG_GROUP_OF[(k, piece, kind)]
        return remote(block, block, ag_s.at[u, k], ag_r.at[u, sem], along(order[k], step))

    def ag_send(u, k, piece):
        ag(u, k, piece, 0).start()
        ag(u, k, piece, 1).start()

    def blocks_of(ref, k, n, cols):
        ix = [0, 0, 0, pl.ds(0, ROWS), pl.ds(0, cols)]
        if k > 0:
            ix[3 - k] = pl.ds(0, n)
            for j in range(4 - k, 3):
                ix[j] = pl.ds(0, SIDE)
        return ref.at[tuple(ix)]

    def ag_got(u, i):
        k, _, kind = AG_GROUPS[i][0]
        n = len(AG_GROUPS[i])
        if k == 0:
            n = 1
        ref = blocks_of(G[u], max(k, 1), n, gathered_width(u))
        remote(ref, ref, ag_s.at[u, k], ag_r.at[u, i], sibling).wait_recv()

    def ag_pass(u, k, piece):
        ag(u, k, piece, 2).start()

    def ag_left(u, k):
        ref = blocks_of(G[u], k + 1, 3, gathered_width(u))
        remote(ref, ref, ag_s.at[u, k], ag_r.at[u, 0], sibling).wait_send()

    def ag_block(u, j):
        order = UNITS[u][0]
        ix = list(part(order, 2, 0, 0, gathered_width(u)))
        ix[order[0]] = at(order[0], j)
        block = G[u].at[tuple(ix)]
        for kind, step in ((0, 1), (1, -1)):
            sem = AG_GROUP_OF[(2, 0, kind)]
            remote(block, block, ag_s.at[u, 2], ag_r.at[u, sem], along(order[2], step)).start()

    def line_a(u):
        ag_got(u, 0)
        ag_pass(u, 0, 0)
        ag_send(u, 1, -1)
        ag_got(u, 1)
        ag_pass(u, 0, 1)
        ag_send(u, 1, 1)

    def line_b(u):
        ag_got(u, 2)
        ag_send(u, 1, 2)
        ag_block(u, 2)

    def plane_a(u):
        ag_got(u, 3)
        ag_pass(u, 1, 0)
        ag_pass(u, 1, -1)
        ag_got(u, 4)
        ag_pass(u, 1, 1)
        ag_pass(u, 1, 2)

    def plane_b(u):
        ag_got(u, 5)
        ag_send(u, 2, -1)
        ag_got(u, 6)
        ag_send(u, 2, 1)

    def plane_c(u):
        ag_got(u, 7)
        ag_send(u, 2, 2)
        hand(u, None, 0).start()

    def cube_a(u, piece):
        ag_got(u, {0: 8, -1: 9, 1: 10, 2: 11}[piece])
        ag_pass(u, 2, piece)
        hand(u, piece, -1).start()
        hand(u, piece, 1).start()

    def cube_b(u, i):
        ag_got(u, 12 + i)
        for r, q in FAR[2 * i : 2 * i + 2]:
            hand(u, r, q).start()

    def hand(u, piece, q):
        order, _, cols = UNITS[u]
        block = part(order, 2, q, piece, cols)
        (i,) = (i for i, rows in enumerate(HAND_GROUPS) if (piece, q) in rows)
        return remote(G[u].at[block], O[u].at[block], as_s.at[u], as_r.at[u, i], sibling)

    def gate_up(u, src, first0, rows):
        order, first, cols = UNITS[u]
        if rows is FAR:
            rows = ((None, 2),)
        ws = pl.ds(pl.multiple_of(first0 + first, LANES), cols)
        if len(rows) == 1:
            lhs = src[part(order, 2, rows[0][1], None, cols)].reshape(256, cols)
            at_a = part(order, 2, rows[0][1], None, GU)
            acc[at_a] = acc[at_a] + dot(lhs, gu[ws, :]).reshape(SIDE, SIDE, ROWS, GU)
            return
        lhs = jnp.concatenate([src[part(order, 2, q, r, cols)].reshape(64, cols) for r, q in rows], axis=0)
        got = dot(lhs, gu[ws, :])
        for i, (r, q) in enumerate(rows):
            at_a = part(order, 2, q, r, GU)
            acc[at_a] = acc[at_a] + got[i * 64 : (i + 1) * 64].reshape(SIDE, ROWS, GU)

    def from_sibling(u, rows):
        n = SIDE if rows is HERE else len(rows)
        ref = blocks_of(O[u], 2, n, UNITS[u][2])
        remote(ref, ref, as_s.at[u], as_r.at[u, HAND_GROUPS.index(rows)], sibling).wait_recv()
        gate_up(u, O[u], other0, rows)

    def shared(u, src, first0):
        _, first, cols = UNITS[u]
        ws = pl.ds(pl.multiple_of(first0 + first, LANES), cols)
        acc_s[...] += dot(src[x, pl.ds(2 * c, 2), :, :, pl.ds(0, cols)].reshape(128, cols), sgu[ws, :])

    def merge_up(first, n):
        def body(i, carry):
            kb = first + i * 4
            ab = dot_t(in_v[:, :, pl.ds(pl.multiple_of(kb * QB, QB), 4 * QB)].reshape(96, 4 * QB), out_bd[...])
            for t in range(4):
                ks = pl.ds(pl.multiple_of(kb * QB, QB) + t * QB, QB)
                for j in range(6):
                    cs = pl.ds(j * LANES, LANES)
                    s = (gate_s if j < 3 else up_s)[j % 3, 0, kb + t]
                    add = ab[t * QB : (t + 1) * QB, j * LANES : (j + 1) * LANES]
                    gu[ks, cs] = (gu[ks, cs].astype(F32) * s + add).astype(BF16)
            return carry

        lax.fori_loop(0, n, body, 0)

    def merge_down(first, n):
        def body(i, carry):
            n0 = pl.multiple_of((first + i) * 1024, 1024)
            ab = dot_t(a_bd[...], b_v[:, :, pl.ds(n0, 1024)].reshape(48, 1024))
            for e in range(3):
                for t in range(8):
                    at_d = (pl.ds(e * LANES, LANES), pl.ds(n0 + t * QB, QB))
                    s = down_s[e, 0, (first + i) * 8 + t]
                    add = ab[e * LANES : (e + 1) * LANES, t * QB : (t + 1) * QB]
                    dcat[at_d] = (dcat[at_d].astype(F32) * s + add).astype(BF16)
            return carry

        lax.fori_loop(0, n, body, 0)

    def wait_w(i):
        wait_all(gu.at[pl.ds(*w_rows[i])], w_sem.at[i])

    ALL = range(NU)
    for u in ALL:
        ag_send(u, 0, 0)
    for u in ALL:
        ag_send(u, 1, 0)
    for u in ALL:
        ag_block(u, 0)
    acc[...] = jnp.zeros_like(acc)
    acc_s[...] = jnp.zeros_like(acc_s)
    m_copy(0).wait()
    wait_w(0)
    merge_up(c * 28, 2)
    for u in ALL:
        line_a(u)
    for u in ALL:
        ag_block(u, -1)
        ag_block(u, 1)
    merge_up(c * 28 + 8, 1)
    wait_w(1)
    merge_up(c * 28 + 12, 2)
    for u in ALL:
        line_b(u)
    merge_up(c * 28 + 20, 2)
    wait_w(2)
    merge_up(o * 28, 1)
    for u in ALL:
        plane_a(u)
    merge_up(o * 28 + 4, 3)
    for u in ALL:
        plane_b(u)
    merge_up(o * 28 + 16, 3)
    m_copy(3).wait()
    wait_all(dcat, m_sem.at[3])
    merge_down(0, 2)
    for u in ALL:
        plane_c(u)
    for u in ALL:
        gate_up(u, G[u], mine0, HERE)
    for u in ALL:
        cube_a(u, 0)
    for u in ALL:
        from_sibling(u, HERE)
    for u in ALL:
        cube_a(u, -1)
    merge_down(2, 2)
    for u in ALL:
        gate_up(u, G[u], mine0, NEAR_A)
    for u in ALL:
        cube_a(u, 1)
    for u in ALL:
        from_sibling(u, NEAR_A)
    for u in ALL:
        cube_a(u, 2)
    for u in ALL:
        gate_up(u, G[u], mine0, NEAR_B)
    merge_down(4, 3)
    for u in ALL:
        from_sibling(u, NEAR_B)
    wait_all(sgu, m_sem.at[1])
    for u in ALL:
        cube_b(u, 0)
    for u in ALL:
        for k in (0, 1):
            ag_left(u, k)
    for u in ALL:
        cube_b(u, 1)
    for u in ALL:
        gate_up(u, G[u], mine0, FAR)
    for u in ALL:
        shared(u, G[u], mine0)
    for u in ALL:
        from_sibling(u, FAR)
        shared(u, O[u], other0)

    choose = (
        lax.broadcasted_iota(jnp.int32, (LANES, HID), 0)
        == lax.broadcasted_iota(jnp.int32, (LANES, HID), 1) // LANES + g * 3
    ).astype(BF16)
    pick_cols = pl.ds(UNITS[PICK_UNIT][2], LANES)

    def silu(v):
        return 0.5 * v * (1.0 + jnp.tanh(0.5 * v))

    def activate(i, carry):
        gate = acc[i, :, :, :, pl.ds(0, HID)].reshape(256, HID)
        up = acc[i, :, :, :, pl.ds(HID, HID)].reshape(256, HID)
        picks = dot(G[PICK_UNIT][i, :, :, :, pick_cols].reshape(256, LANES), choose)
        hcat[i, :, :, :, pl.ds(0, HID)] = (silu(gate) * up * picks).astype(BF16).reshape(SIDE, SIDE, ROWS, HID)
        return carry

    lax.fori_loop(0, SIDE, activate, 0)
    sg = acc_s[:, pl.ds(0, LANES)]
    su = acc_s[:, pl.ds(LANES, LANES)]
    hcat[x, pl.ds(2 * c, 2), :, :, pl.ds(HID, LANES)] = (
        (silu(sg) * su).astype(BF16).reshape(2, SIDE, ROWS, LANES)
    )

    def rows_of(u, q):
        return hcat[part(UNITS[u][0], 2, q, None, DOWN)].reshape(256, DOWN)

    def give(u, r, q):
        order, _, cols = UNITS[u]
        block = part(order, 2, q, r, cols)
        (i,) = (i for i, rows in enumerate(GIVE_GROUPS) if (r, q) in rows)
        return remote(O[u].at[block], S[u].at[block], ss_s.at[u], ss_r.at[u, i], sibling)

    def down_other(u, q):
        order, first, cols = UNITS[u]
        ns = pl.ds(pl.multiple_of(other0 + first, LANES), cols)
        theirs = dot(rows_of(u, q), dcat[:, ns]).astype(BF16)
        O[u][part(order, 2, q, None, cols)] = theirs.reshape(SIDE, SIDE, ROWS, cols)

    def down_mine(u, q):
        order, first, cols = UNITS[u]
        ns = pl.ds(pl.multiple_of(mine0 + first, LANES), cols)
        mine = dot(rows_of(u, q), dcat[:, ns]).astype(BF16)
        G[u][part(order, 2, q, None, cols)] = mine.reshape(SIDE, SIDE, ROWS, cols)

    def take_in(u, i):
        order, _, cols = UNITS[u]
        ref = blocks_of(S[u], 2, len(GIVE_GROUPS[i]), cols)
        remote(ref, ref, ss_s.at[u], ss_r.at[u, i], sibling).wait_recv()
        for r, q in GIVE_GROUPS[i]:
            block = part(order, 2, q, r, cols)
            G[u][block] = G[u][block] + S[u][block]

    def rs_part(k, q, piece, h, order, cols):
        ix = part(order, k, q, piece if k else None, cols)
        return (*ix[:4], halved(cols, h))

    def rs_land(slot, k, piece, h, order, cols):
        ix = landing(slot, order, k, piece if k else None, at, cols)
        return (*ix[:-1], halved(cols, h))

    def rs_sem(k, piece, kind):
        return (2 - k) * 8 + REL.index(piece) * 2 + min(kind, 1)

    def rs(u, k, piece, kind, step):
        order, _, cols = UNITS[u]
        h = 0 if (step == 1) == (kind != 1) else 1
        slot = 0 if kind == 0 else (1 if step == 1 else 2)
        src = G[u].at[rs_part(k, 2 if kind == 0 else step, piece, h, order, cols)]
        dst = R[u][k].at[rs_land(slot, k, piece, h, order, cols)]
        return remote(src, dst, rs_s.at[u, k], rs_r.at[u, rs_sem(k, piece, kind)], along(order[k], step))

    def rs_far(u, k, piece):
        rs(u, k, piece, 0, 1).start()
        rs(u, k, piece, 0, -1).start()

    def rs_near(u, k, piece, step):
        rs(u, k, piece, 1, step).start()

    def rs_got(u, k, piece, kind):
        ref = blocks_of(G[u], max(k, 1), 2 if kind else 1, UNITS[u][2])
        remote(ref, ref, rs_s.at[u, k], rs_r.at[u, rs_sem(k, piece, kind)], sibling).wait_recv()

    def rs_pass(u, k, piece):
        order, _, cols = UNITS[u]
        rs_got(u, k, piece, 0)
        for h, step in ((0, 1), (1, -1)):
            block = rs_part(k, step, piece, h, order, cols)
            came = R[u][k][rs_land(0, k, piece, h, order, cols)]
            G[u][block] = G[u][block] + came
            rs(u, k, piece, 2, step).start()

    def rs_last(u, step):
        order, _, cols = UNITS[u]
        src = G[u].at[part(order, 0, step, None, cols)]
        dst = R[u][0].at[landing({2: 0, 1: 1, -1: 2}[step], order, 0, None, at, cols)]
        remote(src, dst, rs_s.at[u, 0], rs_r.at[u, 16], along(order[0], step)).start()

    def rs_end(u):
        order, _, cols = UNITS[u]
        ref = blocks_of(G[u], 1, 3, cols)
        remote(ref, ref, rs_s.at[u, 0], rs_r.at[u, 16], sibling).wait_recv()
        f, l, r = (R[u][0][landing(i, order, 0, None, at, cols)].astype(F32) for i in range(3))
        return G[u][part(order, 0, 0, None, cols)].astype(F32) + f + (l + r)

    def rs_sum(u, k, piece):
        order, _, cols = UNITS[u]
        rs_got(u, k, piece, 1)
        block = rs_part(k, 0, piece, None, order, cols)
        l = R[u][k][rs_land(1, k, piece, None, order, cols)]
        r = R[u][k][rs_land(2, k, piece, None, order, cols)]
        G[u][block] = (G[u][block].astype(F32) + (l.astype(F32) + r.astype(F32))).astype(BF16)
        if k == 1 and piece != 0:
            rs_last(u, piece)
        elif k == 2:
            for p in (2, 1, -1, 0):
                if piece == 2:
                    rs_far(u, 1, p)
                elif piece != 0:
                    rs_near(u, 1, p, piece)

    for u in ALL:
        down_other(u, 2)
        give(u, 2, 2).start()
        give(u, 1, 2).start()
    for u in ALL:
        ag_left(u, 2)
        ref = G[u].at[:, :, :, :, pl.ds(0, UNITS[u][2])]
        remote(ref, ref, as_s.at[u], as_r.at[u, 0], sibling).wait_send()
    for u in ALL:
        down_mine(u, 2)
        take_in(u, 0)
        rs_far(u, 2, 2)
        take_in(u, 1)
        rs_far(u, 2, 1)
    for u in ALL:
        give(u, -1, 2).start()
        give(u, 0, 2).start()
    for q in (1, -1):
        for u in ALL:
            down_other(u, q)
            give(u, 2, q).start()
            give(u, 1, q).start()
    for u in ALL:
        take_in(u, 2)
        rs_far(u, 2, -1)
    for u in ALL:
        down_mine(u, 1)
        down_mine(u, -1)
        take_in(u, 3)
        rs_near(u, 2, 2, 1)
        rs_near(u, 2, 2, -1)
    for u in ALL:
        for r, q in GIVE_GROUPS[5][1:]:
            give(u, r, q).start()
    for u in ALL:
        rs_pass(u, 2, 2)
        take_in(u, 4)
        rs_near(u, 2, 1, 1)
        rs_near(u, 2, 1, -1)
    for u in ALL:
        for r, q in GIVE_GROUPS[6]:
            give(u, r, q).start()
    for u in ALL:
        down_other(u, 0)
        for r, q in GIVE_GROUPS[7]:
            give(u, r, q).start()
    for u in ALL:
        rs_pass(u, 2, 1)
        take_in(u, 5)
        rs_far(u, 2, 0)
        rs_near(u, 2, -1, 1)
        rs_near(u, 2, -1, -1)
    for u in ALL:
        down_mine(u, 0)
        take_in(u, 7)
    for u in ALL:
        rs_sum(u, 2, 2)
    for u in ALL:
        rs_pass(u, 2, -1)
        take_in(u, 6)
        rs_near(u, 2, 0, 1)
        rs_near(u, 2, 0, -1)
    for u in ALL:
        rs_sum(u, 2, 1)
    for u in ALL:
        rs_pass(u, 2, 0)
    for u in ALL:
        rs_sum(u, 2, -1)
    for p in (2, 1, -1, 0):
        for u in ALL:
            rs_pass(u, 1, p)
    for u in ALL:
        rs_sum(u, 2, 0)
    for p in (2, 1, -1):
        for u in ALL:
            rs_sum(u, 1, p)
    for u in ALL:
        rs_sum(u, 1, 0)
    for u in ALL:
        _, first, cols = UNITS[u]
        fs[:, :, pl.ds(first, cols)] = rs_end(u).reshape(2, 8, cols)

    final = remote(fs.at[o], fr, x_sem.at[2], x_sem.at[3], sibling)
    final.start()
    out[:, pl.ds(pl.multiple_of(mine0, LANES), HALF)] = fs[c].astype(BF16)
    final.wait_recv()
    out[:, pl.ds(pl.multiple_of(other0, LANES), HALF)] = fr[...].astype(BF16)
    final.wait_send()
    for u in ALL:
        for k in range(3):
            ref = blocks_of(G[u], k + 1, 3, UNITS[u][2])
            remote(ref, ref, rs_s.at[u, k], rs_r.at[u, 0], sibling).wait_send()
        remote(O[u], O[u], ss_s.at[u], ss_r.at[u, 0], sibling).wait_send()


def on_device(
    tokens,
    picked_group_index,
    picked_expert_index,
    routing_pick_weight,
    common_gate_weight,
    common_up_weight,
    common_down_weight,
    routed_gate_weight,
    routed_up_weight,
    routed_down_weight,
    gate_block_scales,
    up_block_scales,
    down_block_scales,
    adapter_input_maps,
    adapter_output_maps,
    adapter_down_input,
    adapter_down_output,
):
    vmem = pl.BlockSpec(memory_space=pltpu.VMEM)
    hbm = pl.BlockSpec(memory_space=pl.ANY)
    scratch = []
    for u in range(NU):
        scratch.append(pltpu.VMEM((SIDE, SIDE, SIDE, ROWS, gathered_width(u)), BF16))
    for _ in range(2):
        for _, _, cols in UNITS:
            scratch.append(pltpu.VMEM((SIDE, SIDE, SIDE, ROWS, cols), BF16))
    for _, _, cols in UNITS:
        for k in range(3):
            scratch.append(pltpu.VMEM((3, *([SIDE] * k), ROWS, cols), BF16))
    scratch += [
        pltpu.VMEM((WIDTH, GU), BF16),
        pltpu.VMEM((WIDTH, 2 * LANES), BF16),
        pltpu.VMEM((DOWN, WIDTH), BF16),
        pltpu.VMEM((3, 32, WIDTH), BF16),
        pltpu.VMEM((3, 16, WIDTH), BF16),
        pltpu.VMEM((SIDE, SIDE, SIDE, ROWS, GU), F32),
        pltpu.VMEM((128, 2 * LANES), F32),
        pltpu.VMEM((SIDE, SIDE, SIDE, ROWS, DOWN), BF16),
        pltpu.VMEM((96, GU), BF16),
        pltpu.VMEM((48, HID), BF16),
        pltpu.VMEM((8, HALF + LANES), F32),
        pltpu.VMEM((2, 8, HALF + LANES), F32),
        pltpu.VMEM((2, 8, HALF), F32),
        pltpu.VMEM((8, HALF), F32),
        pltpu.SMEM((3, 1, WIDTH // QB), F32),
        pltpu.SMEM((3, 1, WIDTH // QB), F32),
        pltpu.SMEM((3, 1, WIDTH // QB), F32),
        pltpu.VMEM((8, WIDTH), BF16),
        pltpu.VMEM((8, 8), jnp.int32),
        pltpu.VMEM((8, 8), BF16),
        pltpu.VMEM((3, 2, 16, LANES), BF16),
        pltpu.VMEM((3, 16, LANES), BF16),
        pltpu.SemaphoreType.DMA((8,)),
        pltpu.SemaphoreType.DMA((3,)),
        pltpu.SemaphoreType.DMA((4,)),
        pltpu.SemaphoreType.DMA((4,)),
        pltpu.SemaphoreType.DMA((NU, 3)),
        pltpu.SemaphoreType.DMA((NU, AG_WAITS)),
        pltpu.SemaphoreType.DMA((NU,)),
        pltpu.SemaphoreType.DMA((NU, 4)),
        pltpu.SemaphoreType.DMA((NU, 3)),
        pltpu.SemaphoreType.DMA((NU, 17)),
        pltpu.SemaphoreType.DMA((NU,)),
        pltpu.SemaphoreType.DMA((NU, 8)),
    ]
    return pl.pallas_call(
        kernel,
        out_shape=jax.ShapeDtypeStruct((8, WIDTH), BF16),
        in_specs=[hbm] * 16,
        out_specs=vmem,
        scratch_shapes=scratch,
        compiler_params=pltpu.CompilerParams(
            collective_id=0, has_side_effects=True, vmem_limit_bytes=62 * 2**20
        ),
        cost_estimate=pl.CostEstimate(flops=22 * 10**9, bytes_accessed=25 * 10**6, transcendentals=10**6),
    )(
        gate_block_scales.transpose(0, 2, 1),
        up_block_scales.transpose(0, 2, 1),
        down_block_scales,
        tokens,
        picked_expert_index,
        routing_pick_weight,
        adapter_output_maps,
        adapter_down_input.transpose(0, 2, 1),
        routed_gate_weight,
        routed_up_weight,
        routed_down_weight,
        common_gate_weight,
        common_up_weight,
        common_down_weight,
        adapter_input_maps.transpose(0, 2, 1),
        adapter_down_output,
    )


def solution(mesh):
    in_specs = (
        P(("group", "local"), None),
        P(("group", "local"), None),
        P(("group", "local"), None),
        P(("group", "local"), None),
        P(None, "local"),
        P(None, "local"),
        P("local", None),
        P("group", None, "local"),
        P("group", None, "local"),
        P("group", "local", None),
        P("group", None, "local"),
        P("group", None, "local"),
        P("group", "local", None),
        P("group", None, None),
        P("group", None, None, "local"),
        P("group", "local", None),
        P("group", None, None),
    )
    return jax.shard_map(
        on_device, mesh=mesh, in_specs=in_specs, out_specs=P(("group", "local"), None), check_vma=False
    )
```

```python
import functools

import jax
import jax.numpy as jnp
from jax import lax
from jax.experimental import pallas as pl
from jax.experimental.pallas import tpu as pltpu
from jax.sharding import PartitionSpec as P

MESH = pl.DeviceIdType.MESH
F32 = jnp.float32
BF16 = jnp.bfloat16

WIDTH = 7168
HALF = WIDTH // 2
SIDE = 4
ROWS = 16
QB = 128
LANES = 128
HID = 384
GU = 2 * HID
DOWN = HID + LANES

UNITS = (
    ((0, 1, 2), 0, 1280),
    ((1, 2, 0), 1280, 1280),
    ((2, 0, 1), 2560, 1024),
)
NU = len(UNITS)
PICK_UNIT = 2
REL = (0, 1, -1, 2)

AG_GROUPS = (
    ((0, 0, 0),),
    ((0, 0, 1),),
    ((0, 0, 2), (0, 1, 2)),
    ((1, 0, 0), (1, -1, 1)),
    ((1, 1, 0), (1, 2, 1)),
    ((1, -1, 0), (1, 2, 0)),
    ((1, 0, 1), (1, 1, 1)),
    ((1, 0, 2), (1, 1, 2), (1, -1, 2), (1, 2, 2)),
    ((2, 0, 0), (2, 0, 1)),
    ((2, -1, 0), (2, -1, 1)),
    ((2, 1, 0), (2, 1, 1)),
    ((2, 2, 0), (2, 2, 1)),
    ((2, 0, 2), (2, -1, 2)),
    ((2, 1, 2), (2, 2, 2)),
)
AG_WAITS = len(AG_GROUPS)
AG_GROUP_OF = {copy: i for i, group in enumerate(AG_GROUPS) for copy in group}
HERE = ((None, 0),)
NEAR_A = ((0, -1), (0, 1), (-1, -1), (-1, 1))
NEAR_B = ((1, -1), (1, 1), (2, -1), (2, 1))
FAR = ((0, 2), (-1, 2), (1, 2), (2, 2))
HAND_GROUPS = (HERE, NEAR_A, NEAR_B, FAR)
GIVE_GROUPS = (
    ((2, 2),),
    ((1, 2),),
    ((-1, 2),),
    ((2, 1), (2, -1)),
    ((1, 1), (1, -1)),
    ((0, 2), (-1, 1), (-1, -1)),
    ((0, 1), (0, -1)),
    ((2, 0), (1, 0), (-1, 0), (0, 0)),
)


def gathered_width(u):
    return UNITS[u][2] + (LANES if u == PICK_UNIT else 0)


def halved(cols, h):
    if h is None:
        return pl.ds(0, cols)
    cut = cols // 256 * LANES
    return pl.ds(0, cut) if h == 0 else pl.ds(cut, cols - cut)


def landing(slot, order, k, piece, at, cols):
    if k == 0:
        return (slot, pl.ds(0, ROWS), halved(cols, piece))
    whole = sorted(order[:k])
    ix = [pl.ds(0, SIDE)] * k
    if piece is not None:
        ix[whole.index(order[k - 1])] = at(order[k - 1], piece)
    return (slot, *ix, pl.ds(0, ROWS), pl.ds(0, cols))


def dot(a, b):
    return jnp.dot(a, b, preferred_element_type=F32)


def dot_t(a, b):
    return lax.dot_general(a, b, (((0,), (0,)), ((), ())), preferred_element_type=F32)


def kernel(*refs):
    it = iter(refs)

    def take(n):
        return [next(it) for _ in range(n)]

    small_in = take(8)
    (gate_w, up_w, down_w, sgate_w, sup_w, sdown_w, in_t, b_maps) = take(8)
    (out,) = take(1)
    G = take(NU)
    O = take(NU)
    S = take(NU)
    R = [take(3) for _ in range(NU)]
    (gu, sgu, dcat, in_v, b_v, acc, acc_s, hcat, out_bd, a_bd, xs, xf, fs, fr) = take(14)
    small = take(8)
    (gate_s, up_s, down_s, tokens, picked, weight, out_maps, a_t) = small
    (i_sem, w_sem, m_sem, x_sem, ag_s, ag_r, as_s, as_r, rs_s, rs_r, ss_s, ss_r) = take(12)

    g = lax.axis_index("group")
    loc = lax.axis_index("local")
    x, c = g // 2, g % 2
    z, y = loc // SIDE, loc % SIDE
    own = (x, y, z)
    o = 1 - c

    def along(axis, step):
        p = (own[axis] + step + SIDE) % SIDE
        if axis == 0:
            return (p * 2 + c, loc)
        if axis == 1:
            return (g, z * SIDE + p)
        return (g, p * SIDE + y)

    sibling = (x * 2 + o, loc)

    def at(axis, step):
        return (own[axis] + step + SIDE) % SIDE

    def part(order, k, q, piece, cols):
        ix = list(own)
        for a in order[:k]:
            ix[a] = pl.ds(0, SIDE)
        ix[order[k]] = at(order[k], q)
        if k == 0:
            return (*ix, pl.ds(0, ROWS), halved(cols, piece))
        if piece is not None:
            ix[order[k - 1]] = at(order[k - 1], piece)
        return (*ix, pl.ds(0, ROWS), pl.ds(0, cols))

    def remote(src, dst, ss, rs, dev):
        return pltpu.make_async_remote_copy(
            src_ref=src, dst_ref=dst, send_sem=ss, recv_sem=rs, device_id=dev, device_id_type=MESH
        )

    barrier = pltpu.get_barrier_semaphore()
    partners = [along(a, s) for a in range(3) for s in (1, -1, 2)] + [sibling]
    for p in partners:
        pl.semaphore_signal(barrier, inc=1, device_id=p, device_id_type=MESH)

    inward = [pltpu.make_async_copy(a, b, i_sem.at[i]) for i, (a, b) in enumerate(zip(small_in, small))]
    for i in (3, 4, 5, 6, 7, 0, 1, 2):
        inward[i].start()
    mine0 = c * HALF
    other0 = o * HALF
    w_rows = ((mine0, HALF // 2), (mine0 + HALF // 2, HALF // 2), (other0, HALF))

    def w_copy(i, j):
        rows = pl.ds(*w_rows[i])
        src = (gate_w if j < 3 else up_w).at[j % 3, rows]
        return pltpu.make_async_copy(src, gu.at[rows, pl.ds(j * LANES, LANES)], w_sem.at[i])

    def m_copy(i):
        if i == 0:
            return pltpu.make_async_copy(in_t, in_v, m_sem.at[0])
        if i < 3:
            src = sgate_w if i == 1 else sup_w
            return pltpu.make_async_copy(src, sgu.at[:, pl.ds((i - 1) * LANES, LANES)], m_sem.at[1])
        if i == 3:
            return pltpu.make_async_copy(b_maps, b_v, m_sem.at[2])
        if i == 4:
            return pltpu.make_async_copy(sdown_w, dcat.at[pl.ds(HID, LANES)], m_sem.at[3])
        return pltpu.make_async_copy(down_w.at[i - 5], dcat.at[pl.ds((i - 5) * LANES, LANES)], m_sem.at[3])

    def wait_all(ref, sem):
        pltpu.make_async_copy(ref, ref, sem).wait()

    m_copy(0).start()
    for j in range(6):
        w_copy(0, j).start()

    out_bd[...] = jnp.zeros_like(out_bd)
    a_bd[...] = jnp.zeros_like(a_bd)
    hcat[:, :, :, :, pl.ds(HID, LANES)] = jnp.zeros((SIDE, SIDE, SIDE, ROWS, LANES), BF16)
    for i in (3, 4, 5):
        inward[i].wait()
    lane = lax.broadcasted_iota(jnp.int32, (8, LANES), 1)
    pick = jnp.zeros((8, LANES), F32)
    for k in range(8):
        pick = pick + jnp.where(lane == picked[:, k : k + 1], weight[:, k : k + 1].astype(F32), 0.0)
    xs[:, pl.ds(0, HALF)] = tokens[:, pl.ds(pl.multiple_of(other0, LANES), HALF)].astype(F32)
    xs[:, pl.ds(HALF, LANES)] = pick
    xf[c, :, pl.ds(0, HALF)] = tokens[:, pl.ds(pl.multiple_of(mine0, LANES), HALF)].astype(F32)
    xf[c, :, pl.ds(HALF, LANES)] = pick
    pl.semaphore_wait(barrier, len(partners))
    swap = remote(xs, xf.at[c], x_sem.at[0], x_sem.at[1], sibling)
    swap.start()

    for i in (1, 2):
        for j in range(6):
            w_copy(i, j).start()
    for i in range(1, 8):
        m_copy(i).start()
    for i in (6, 7, 0, 1, 2):
        inward[i].wait()
    for e in range(3):
        for h in range(2):
            out_bd[pl.ds(e * 32 + h * 16, 16), pl.ds((h * 3 + e) * LANES, LANES)] = out_maps[e, h]
        a_bd[pl.ds(e * 16, 16), pl.ds(e * LANES, LANES)] = a_t[e]
    swap.wait_send()
    remote(xs, xf.at[o], x_sem.at[0], x_sem.at[1], sibling).wait_recv()
    block = xf[...].reshape(ROWS, HALF + LANES).astype(BF16)
    for u, (order, first, cols) in enumerate(UNITS):
        G[u][x, y, z, :, pl.ds(0, cols)] = block[:, first : first + cols]
        if u == PICK_UNIT:
            G[u][x, y, z, :, pl.ds(cols, LANES)] = block[:, HALF:]

    def ag(u, k, piece, kind, arriving=False):
        order = UNITS[u][0]
        if kind == 2:
            step = 1 if piece in ((0,) if k == 0 else (0, 1)) else -1
            q = -2 * step if arriving else -step
        else:
            step = 1 if kind == 0 else -1
            q = -step if arriving else 0
        which = None if k == 0 and kind < 2 else piece
        block = G[u].at[part(order, k, q, which, gathered_width(u))]
        sem = AG_GROUP_OF[(k, piece, kind)]
        return remote(block, block, ag_s.at[u, k], ag_r.at[u, sem], along(order[k], step))

    def ag_send(u, k, piece):
        ag(u, k, piece, 0).start()
        ag(u, k, piece, 1).start()

    def blocks_of(ref, k, n, cols):
        ix = [0, 0, 0, pl.ds(0, ROWS), pl.ds(0, cols)]
        if k > 0:
            ix[3 - k] = pl.ds(0, n)
            for j in range(4 - k, 3):
                ix[j] = pl.ds(0, SIDE)
        return ref.at[tuple(ix)]

    def ag_got(u, i):
        k, _, kind = AG_GROUPS[i][0]
        n = len(AG_GROUPS[i])
        if k == 0:
            n = 1
        ref = blocks_of(G[u], max(k, 1), n, gathered_width(u))
        remote(ref, ref, ag_s.at[u, k], ag_r.at[u, i], sibling).wait_recv()

    def ag_pass(u, k, piece):
        ag(u, k, piece, 2).start()

    def ag_left(u, k):
        ref = blocks_of(G[u], k + 1, 3, gathered_width(u))
        remote(ref, ref, ag_s.at[u, k], ag_r.at[u, 0], sibling).wait_send()

    def ag_block(u, j):
        order = UNITS[u][0]
        ix = list(part(order, 2, 0, 0, gathered_width(u)))
        ix[order[0]] = at(order[0], j)
        block = G[u].at[tuple(ix)]
        for kind, step in ((0, 1), (1, -1)):
            sem = AG_GROUP_OF[(2, 0, kind)]
            remote(block, block, ag_s.at[u, 2], ag_r.at[u, sem], along(order[2], step)).start()

    def line_a(u):
        ag_got(u, 0)
        ag_pass(u, 0, 0)
        ag_send(u, 1, -1)
        ag_got(u, 1)
        ag_pass(u, 0, 1)
        ag_send(u, 1, 1)

    def line_b(u):
        ag_got(u, 2)
        ag_send(u, 1, 2)
        ag_block(u, 2)

    def plane_a(u):
        ag_got(u, 3)
        ag_pass(u, 1, 0)
        ag_pass(u, 1, -1)
        ag_got(u, 4)
        ag_pass(u, 1, 1)
        ag_pass(u, 1, 2)

    def plane_b(u):
        ag_got(u, 5)
        ag_send(u, 2, -1)
        ag_got(u, 6)
        ag_send(u, 2, 1)

    def plane_c(u):
        ag_got(u, 7)
        ag_send(u, 2, 2)
        hand(u, None, 0).start()

    def cube_a(u, piece):
        ag_got(u, {0: 8, -1: 9, 1: 10, 2: 11}[piece])
        ag_pass(u, 2, piece)
        hand(u, piece, -1).start()
        hand(u, piece, 1).start()

    def cube_b(u, i):
        ag_got(u, 12 + i)
        for r, q in FAR[2 * i : 2 * i + 2]:
            hand(u, r, q).start()

    def hand(u, piece, q):
        order, _, cols = UNITS[u]
        block = part(order, 2, q, piece, cols)
        (i,) = (i for i, rows in enumerate(HAND_GROUPS) if (piece, q) in rows)
        return remote(G[u].at[block], O[u].at[block], as_s.at[u], as_r.at[u, i], sibling)

    def gate_up(u, src, first0, rows):
        order, first, cols = UNITS[u]
        if rows is FAR:
            rows = ((None, 2),)
        ws = pl.ds(pl.multiple_of(first0 + first, LANES), cols)
        if len(rows) == 1:
            lhs = src[part(order, 2, rows[0][1], None, cols)].reshape(256, cols)
            at_a = part(order, 2, rows[0][1], None, GU)
            acc[at_a] = acc[at_a] + dot(lhs, gu[ws, :]).reshape(SIDE, SIDE, ROWS, GU)
            return
        lhs = jnp.concatenate([src[part(order, 2, q, r, cols)].reshape(64, cols) for r, q in rows], axis=0)
        got = dot(lhs, gu[ws, :])
        for i, (r, q) in enumerate(rows):
            at_a = part(order, 2, q, r, GU)
            acc[at_a] = acc[at_a] + got[i * 64 : (i + 1) * 64].reshape(SIDE, ROWS, GU)

    def from_sibling(u, rows, work=True):
        n = SIDE if rows is HERE else len(rows)
        ref = blocks_of(O[u], 2, n, UNITS[u][2])
        remote(ref, ref, as_s.at[u], as_r.at[u, HAND_GROUPS.index(rows)], sibling).wait_recv()
        if work:
            gate_up(u, O[u], other0, rows)

    def shared(u, src, first0):
        _, first, cols = UNITS[u]
        ws = pl.ds(pl.multiple_of(first0 + first, LANES), cols)
        acc_s[...] += dot(src[x, pl.ds(2 * c, 2), :, :, pl.ds(0, cols)].reshape(128, cols), sgu[ws, :])

    def merge_up(first, n):
        def body(i, carry):
            kb = first + i * 4
            ab = dot_t(in_v[:, :, pl.ds(pl.multiple_of(kb * QB, QB), 4 * QB)].reshape(96, 4 * QB), out_bd[...])
            for t in range(4):
                ks = pl.ds(pl.multiple_of(kb * QB, QB) + t * QB, QB)
                for j in range(6):
                    cs = pl.ds(j * LANES, LANES)
                    s = (gate_s if j < 3 else up_s)[j % 3, 0, kb + t]
                    add = ab[t * QB : (t + 1) * QB, j * LANES : (j + 1) * LANES]
                    gu[ks, cs] = (gu[ks, cs].astype(F32) * s + add).astype(BF16)
            return carry

        lax.fori_loop(0, n, body, 0)

    def merge_down(first, n):
        def body(i, carry):
            n0 = pl.multiple_of((first + i) * 1024, 1024)
            ab = dot_t(a_bd[...], b_v[:, :, pl.ds(n0, 1024)].reshape(48, 1024))
            for e in range(3):
                for t in range(8):
                    at_d = (pl.ds(e * LANES, LANES), pl.ds(n0 + t * QB, QB))
                    s = down_s[e, 0, (first + i) * 8 + t]
                    add = ab[e * LANES : (e + 1) * LANES, t * QB : (t + 1) * QB]
                    dcat[at_d] = (dcat[at_d].astype(F32) * s + add).astype(BF16)
            return carry

        lax.fori_loop(0, n, body, 0)

    def wait_w(i):
        wait_all(gu.at[pl.ds(*w_rows[i])], w_sem.at[i])

    ALL = range(NU)
    for u in ALL:
        ag_send(u, 0, 0)
    for u in ALL:
        ag_send(u, 1, 0)
    for u in ALL:
        ag_block(u, 0)
    acc[...] = jnp.zeros_like(acc)
    acc_s[...] = jnp.zeros_like(acc_s)
    m_copy(0).wait()
    wait_w(0)
    merge_up(c * 28, 2)
    for u in ALL:
        line_a(u)
    for u in ALL:
        ag_block(u, -1)
        ag_block(u, 1)
    merge_up(c * 28 + 8, 1)
    wait_w(1)
    merge_up(c * 28 + 12, 2)
    for u in ALL:
        line_b(u)
    merge_up(c * 28 + 20, 2)
    wait_w(2)
    merge_up(o * 28, 1)
    for u in ALL:
        plane_a(u)
    merge_up(o * 28 + 4, 3)
    for u in ALL:
        plane_b(u)
    merge_up(o * 28 + 16, 3)
    m_copy(3).wait()
    wait_all(dcat, m_sem.at[3])
    merge_down(0, 2)
    for u in ALL:
        plane_c(u)
    for u in ALL:
        gate_up(u, G[u], mine0, HERE)
    for u in ALL:
        cube_a(u, 0)
    for u in ALL:
        from_sibling(u, HERE)
    for u in ALL:
        cube_a(u, -1)
    merge_down(2, 2)
    merge_down(4, 3)
    for u in ALL:
        cube_a(u, 1)
    for u in ALL:
        cube_a(u, 2)
    for u in ALL:
        gate_up(u, G[u], mine0, ((None, -1),))
        gate_up(u, G[u], mine0, ((None, 1),))
    for u in ALL:
        from_sibling(u, NEAR_A, False)
        from_sibling(u, NEAR_B, False)
        gate_up(u, O[u], other0, ((None, -1),))
        gate_up(u, O[u], other0, ((None, 1),))
    wait_all(sgu, m_sem.at[1])
    for u in ALL:
        cube_b(u, 0)
    for u in ALL:
        for k in (0, 1):
            ag_left(u, k)
    for u in ALL:
        cube_b(u, 1)
    for u in ALL:
        gate_up(u, G[u], mine0, FAR)
    for u in ALL:
        shared(u, G[u], mine0)
    for u in ALL:
        from_sibling(u, FAR)
        shared(u, O[u], other0)

    choose = (
        lax.broadcasted_iota(jnp.int32, (LANES, HID), 0)
        == lax.broadcasted_iota(jnp.int32, (LANES, HID), 1) // LANES + g * 3
    ).astype(BF16)
    pick_cols = pl.ds(UNITS[PICK_UNIT][2], LANES)

    def silu(v):
        return 0.5 * v * (1.0 + jnp.tanh(0.5 * v))

    def activate(i, carry):
        gate = acc[i, :, :, :, pl.ds(0, HID)].reshape(256, HID)
        up = acc[i, :, :, :, pl.ds(HID, HID)].reshape(256, HID)
        picks = dot(G[PICK_UNIT][i, :, :, :, pick_cols].reshape(256, LANES), choose)
        hcat[i, :, :, :, pl.ds(0, HID)] = (silu(gate) * up * picks).astype(BF16).reshape(SIDE, SIDE, ROWS, HID)
        return carry

    lax.fori_loop(0, SIDE, activate, 0)
    sg = acc_s[:, pl.ds(0, LANES)]
    su = acc_s[:, pl.ds(LANES, LANES)]
    hcat[x, pl.ds(2 * c, 2), :, :, pl.ds(HID, LANES)] = (
        (silu(sg) * su).astype(BF16).reshape(2, SIDE, ROWS, LANES)
    )

    def rows_of(u, q):
        return hcat[part(UNITS[u][0], 2, q, None, DOWN)].reshape(256, DOWN)

    def give(u, r, q):
        order, _, cols = UNITS[u]
        block = part(order, 2, q, r, cols)
        (i,) = (i for i, rows in enumerate(GIVE_GROUPS) if (r, q) in rows)
        return remote(O[u].at[block], S[u].at[block], ss_s.at[u], ss_r.at[u, i], sibling)

    def down_other(u, q):
        order, first, cols = UNITS[u]
        ns = pl.ds(pl.multiple_of(other0 + first, LANES), cols)
        theirs = dot(rows_of(u, q), dcat[:, ns]).astype(BF16)
        O[u][part(order, 2, q, None, cols)] = theirs.reshape(SIDE, SIDE, ROWS, cols)

    def down_mine(u, q):
        order, first, cols = UNITS[u]
        ns = pl.ds(pl.multiple_of(mine0 + first, LANES), cols)
        mine = dot(rows_of(u, q), dcat[:, ns]).astype(BF16)
        G[u][part(order, 2, q, None, cols)] = mine.reshape(SIDE, SIDE, ROWS, cols)

    def down_near(u, first0, dst):
        order, first, cols = UNITS[u]
        ns = pl.ds(pl.multiple_of(first0 + first, LANES), cols)
        lhs = jnp.concatenate([rows_of(u, 1), rows_of(u, -1)], axis=0)
        got = dot(lhs, dcat[:, ns]).astype(BF16)
        for i, q in enumerate((1, -1)):
            dst[u][part(order, 2, q, None, cols)] = got[i * 256 : (i + 1) * 256].reshape(SIDE, SIDE, ROWS, cols)

    def take_in(u, i):
        order, _, cols = UNITS[u]
        ref = blocks_of(S[u], 2, len(GIVE_GROUPS[i]), cols)
        remote(ref, ref, ss_s.at[u], ss_r.at[u, i], sibling).wait_recv()
        for r, q in GIVE_GROUPS[i]:
            block = part(order, 2, q, r, cols)
            G[u][block] = G[u][block] + S[u][block]

    def rs_part(k, q, piece, h, order, cols):
        ix = part(order, k, q, piece if k else None, cols)
        return (*ix[:4], halved(cols, h))

    def rs_land(slot, k, piece, h, order, cols):
        ix = landing(slot, order, k, piece if k else None, at, cols)
        return (*ix[:-1], halved(cols, h))

    def rs_sem(k, piece, kind):
        return (2 - k) * 8 + REL.index(piece) * 2 + min(kind, 1)

    def rs(u, k, piece, kind, step):
        order, _, cols = UNITS[u]
        h = 0 if (step == 1) == (kind != 1) else 1
        slot = 0 if kind == 0 else (1 if step == 1 else 2)
        src = G[u].at[rs_part(k, 2 if kind == 0 else step, piece, h, order, cols)]
        dst = R[u][k].at[rs_land(slot, k, piece, h, order, cols)]
        return remote(src, dst, rs_s.at[u, k], rs_r.at[u, rs_sem(k, piece, kind)], along(order[k], step))

    def rs_far(u, k, piece):
        rs(u, k, piece, 0, 1).start()
        rs(u, k, piece, 0, -1).start()

    def rs_near(u, k, piece, step):
        rs(u, k, piece, 1, step).start()

    def rs_got(u, k, piece, kind):
        ref = blocks_of(G[u], max(k, 1), 2 if kind else 1, UNITS[u][2])
        remote(ref, ref, rs_s.at[u, k], rs_r.at[u, rs_sem(k, piece, kind)], sibling).wait_recv()

    def rs_pass(u, k, piece):
        order, _, cols = UNITS[u]
        rs_got(u, k, piece, 0)
        for h, step in ((0, 1), (1, -1)):
            block = rs_part(k, step, piece, h, order, cols)
            came = R[u][k][rs_land(0, k, piece, h, order, cols)]
            G[u][block] = G[u][block] + came
            rs(u, k, piece, 2, step).start()

    def rs_last(u, step):
        order, _, cols = UNITS[u]
        src = G[u].at[part(order, 0, step, None, cols)]
        dst = R[u][0].at[landing({2: 0, 1: 1, -1: 2}[step], order, 0, None, at, cols)]
        remote(src, dst, rs_s.at[u, 0], rs_r.at[u, 16], along(order[0], step)).start()

    def rs_end(u):
        order, _, cols = UNITS[u]
        ref = blocks_of(G[u], 1, 3, cols)
        remote(ref, ref, rs_s.at[u, 0], rs_r.at[u, 16], sibling).wait_recv()
        f, l, r = (R[u][0][landing(i, order, 0, None, at, cols)].astype(F32) for i in range(3))
        return G[u][part(order, 0, 0, None, cols)].astype(F32) + f + (l + r)

    def rs_sum(u, k, piece):
        order, _, cols = UNITS[u]
        rs_got(u, k, piece, 1)
        block = rs_part(k, 0, piece, None, order, cols)
        l = R[u][k][rs_land(1, k, piece, None, order, cols)]
        r = R[u][k][rs_land(2, k, piece, None, order, cols)]
        G[u][block] = (G[u][block].astype(F32) + (l.astype(F32) + r.astype(F32))).astype(BF16)
        if k == 1 and piece != 0:
            rs_last(u, piece)
        elif k == 2:
            for p in (2, 1, -1, 0):
                if piece == 2:
                    rs_far(u, 1, p)
                elif piece != 0:
                    rs_near(u, 1, p, piece)

    for u in ALL:
        down_other(u, 2)
        give(u, 2, 2).start()
        give(u, 1, 2).start()
    for u in ALL:
        ag_left(u, 2)
        ref = G[u].at[:, :, :, :, pl.ds(0, UNITS[u][2])]
        remote(ref, ref, as_s.at[u], as_r.at[u, 0], sibling).wait_send()
    for u in ALL:
        down_mine(u, 2)
        take_in(u, 0)
        rs_far(u, 2, 2)
        take_in(u, 1)
        rs_far(u, 2, 1)
    for u in ALL:
        give(u, -1, 2).start()
        give(u, 0, 2).start()
    for u in ALL:
        down_near(u, other0, O)
        for r in (2, 1):
            for q in (1, -1):
                give(u, r, q).start()
    for u in ALL:
        take_in(u, 2)
        rs_far(u, 2, -1)
    for u in ALL:
        down_near(u, mine0, G)
        take_in(u, 3)
        rs_near(u, 2, 2, 1)
        rs_near(u, 2, 2, -1)
    for u in ALL:
        for r, q in GIVE_GROUPS[5][1:]:
            give(u, r, q).start()
    for u in ALL:
        rs_pass(u, 2, 2)
        take_in(u, 4)
        rs_near(u, 2, 1, 1)
        rs_near(u, 2, 1, -1)
    for u in ALL:
        for r, q in GIVE_GROUPS[6]:
            give(u, r, q).start()
    for u in ALL:
        down_other(u, 0)
        for r, q in GIVE_GROUPS[7]:
            give(u, r, q).start()
    for u in ALL:
        rs_pass(u, 2, 1)
        take_in(u, 5)
        rs_far(u, 2, 0)
        rs_near(u, 2, -1, 1)
        rs_near(u, 2, -1, -1)
    for u in ALL:
        down_mine(u, 0)
        take_in(u, 7)
    for u in ALL:
        rs_sum(u, 2, 2)
    for u in ALL:
        rs_pass(u, 2, -1)
        take_in(u, 6)
        rs_near(u, 2, 0, 1)
        rs_near(u, 2, 0, -1)
    for u in ALL:
        rs_sum(u, 2, 1)
    for u in ALL:
        rs_pass(u, 2, 0)
    for u in ALL:
        rs_sum(u, 2, -1)
    for p in (2, 1, -1, 0):
        for u in ALL:
            rs_pass(u, 1, p)
    for u in ALL:
        rs_sum(u, 2, 0)
    for p in (2, 1, -1):
        for u in ALL:
            rs_sum(u, 1, p)
    for u in ALL:
        rs_sum(u, 1, 0)
    for u in ALL:
        _, first, cols = UNITS[u]
        fs[:, :, pl.ds(first, cols)] = rs_end(u).reshape(2, 8, cols)

    final = remote(fs.at[o], fr, x_sem.at[2], x_sem.at[3], sibling)
    final.start()
    out[:, pl.ds(pl.multiple_of(mine0, LANES), HALF)] = fs[c].astype(BF16)
    final.wait_recv()
    out[:, pl.ds(pl.multiple_of(other0, LANES), HALF)] = fr[...].astype(BF16)
    final.wait_send()
    for u in ALL:
        for k in range(3):
            ref = blocks_of(G[u], k + 1, 3, UNITS[u][2])
            remote(ref, ref, rs_s.at[u, k], rs_r.at[u, 0], sibling).wait_send()
        remote(O[u], O[u], ss_s.at[u], ss_r.at[u, 0], sibling).wait_send()


def on_device(
    tokens,
    picked_group_index,
    picked_expert_index,
    routing_pick_weight,
    common_gate_weight,
    common_up_weight,
    common_down_weight,
    routed_gate_weight,
    routed_up_weight,
    routed_down_weight,
    gate_block_scales,
    up_block_scales,
    down_block_scales,
    adapter_input_maps,
    adapter_output_maps,
    adapter_down_input,
    adapter_down_output,
):
    vmem = pl.BlockSpec(memory_space=pltpu.VMEM)
    hbm = pl.BlockSpec(memory_space=pl.ANY)
    scratch = []
    for u in range(NU):
        scratch.append(pltpu.VMEM((SIDE, SIDE, SIDE, ROWS, gathered_width(u)), BF16))
    for _ in range(2):
        for _, _, cols in UNITS:
            scratch.append(pltpu.VMEM((SIDE, SIDE, SIDE, ROWS, cols), BF16))
    for _, _, cols in UNITS:
        for k in range(3):
            scratch.append(pltpu.VMEM((3, *([SIDE] * k), ROWS, cols), BF16))
    scratch += [
        pltpu.VMEM((WIDTH, GU), BF16),
        pltpu.VMEM((WIDTH, 2 * LANES), BF16),
        pltpu.VMEM((DOWN, WIDTH), BF16),
        pltpu.VMEM((3, 32, WIDTH), BF16),
        pltpu.VMEM((3, 16, WIDTH), BF16),
        pltpu.VMEM((SIDE, SIDE, SIDE, ROWS, GU), F32),
        pltpu.VMEM((128, 2 * LANES), F32),
        pltpu.VMEM((SIDE, SIDE, SIDE, ROWS, DOWN), BF16),
        pltpu.VMEM((96, GU), BF16),
        pltpu.VMEM((48, HID), BF16),
        pltpu.VMEM((8, HALF + LANES), F32),
        pltpu.VMEM((2, 8, HALF + LANES), F32),
        pltpu.VMEM((2, 8, HALF), F32),
        pltpu.VMEM((8, HALF), F32),
        pltpu.SMEM((3, 1, WIDTH // QB), F32),
        pltpu.SMEM((3, 1, WIDTH // QB), F32),
        pltpu.SMEM((3, 1, WIDTH // QB), F32),
        pltpu.VMEM((8, WIDTH), BF16),
        pltpu.VMEM((8, 8), jnp.int32),
        pltpu.VMEM((8, 8), BF16),
        pltpu.VMEM((3, 2, 16, LANES), BF16),
        pltpu.VMEM((3, 16, LANES), BF16),
        pltpu.SemaphoreType.DMA((8,)),
        pltpu.SemaphoreType.DMA((3,)),
        pltpu.SemaphoreType.DMA((4,)),
        pltpu.SemaphoreType.DMA((4,)),
        pltpu.SemaphoreType.DMA((NU, 3)),
        pltpu.SemaphoreType.DMA((NU, AG_WAITS)),
        pltpu.SemaphoreType.DMA((NU,)),
        pltpu.SemaphoreType.DMA((NU, 4)),
        pltpu.SemaphoreType.DMA((NU, 3)),
        pltpu.SemaphoreType.DMA((NU, 17)),
        pltpu.SemaphoreType.DMA((NU,)),
        pltpu.SemaphoreType.DMA((NU, 8)),
    ]
    return pl.pallas_call(
        kernel,
        out_shape=jax.ShapeDtypeStruct((8, WIDTH), BF16),
        in_specs=[hbm] * 16,
        out_specs=vmem,
        scratch_shapes=scratch,
        compiler_params=pltpu.CompilerParams(
            collective_id=0, has_side_effects=True, vmem_limit_bytes=62 * 2**20
        ),
        cost_estimate=pl.CostEstimate(flops=22 * 10**9, bytes_accessed=25 * 10**6, transcendentals=10**6),
    )(
        gate_block_scales.transpose(0, 2, 1),
        up_block_scales.transpose(0, 2, 1),
        down_block_scales,
        tokens,
        picked_expert_index,
        routing_pick_weight,
        adapter_output_maps,
        adapter_down_input.transpose(0, 2, 1),
        routed_gate_weight,
        routed_up_weight,
        routed_down_weight,
        common_gate_weight,
        common_up_weight,
        common_down_weight,
        adapter_input_maps.transpose(0, 2, 1),
        adapter_down_output,
    )


def solution(mesh):
    in_specs = (
        P(("group", "local"), None),
        P(("group", "local"), None),
        P(("group", "local"), None),
        P(("group", "local"), None),
        P(None, "local"),
        P(None, "local"),
        P("local", None),
        P("group", None, "local"),
        P("group", None, "local"),
        P("group", "local", None),
        P("group", None, "local"),
        P("group", None, "local"),
        P("group", "local", None),
        P("group", None, None),
        P("group", None, None, "local"),
        P("group", "local", None),
        P("group", None, None),
    )
    return jax.shard_map(
        on_device, mesh=mesh, in_specs=in_specs, out_specs=P(("group", "local"), None), check_vma=False
    )
```
